512 devices in a mesh: dp: 16 (over z_lo, core), expert: 32 (over y, z_hi, x).
Axes of the slice: x: 4, y: 4, z: 16 (z_hi: 2, z_lo: 8; z = z_hi * 8 + z_lo), core: 2. Of those that a mesh axis runs over, the one named last changes fastest.
Arguments:
- tokens: bfloat16 [65536, 1024], P(('dp', 'expert')), may hold values from -6 to 6
- cotangent: bfloat16 [65536, 1024], P(('dp', 'expert')), may hold values from -6 to 6
- routing: int32 [65536, 2], P(('dp', 'expert')), may hold values from 0 to 31, all different within a row; in each aligned block of 128 rows (0 to 127, 128 to 255, ...) at most 16 rows name the same one
- gate_values: float32 [65536, 2], P(('dp', 'expert')), may hold values from 0.1 to 1
- live_counts: int32 [512], P(('dp', 'expert')), may hold values from 64 to 128
- gate_weights: bfloat16 [32, 1024, 384], P('expert', 'dp'), may hold values from -0.1875 to 0.1875
- up_weights: bfloat16 [32, 1024, 384], P('expert', 'dp'), may hold values from -0.1875 to 0.1875
- down_weights: bfloat16 [32, 384, 1024], P('expert', 'dp'), may hold values from -0.3125 to 0.3125
Outputs:
- mixed: bfloat16 [65536, 1024], P(('dp', 'expert'))
- token_grad: bfloat16 [65536, 1024], P(('dp', 'expert'))
- gate_grad: float32 [65536, 2], P(('dp', 'expert'))
- grad_gate_w: bfloat16 [32, 1024, 384], P('expert', 'dp')
- grad_up_w: bfloat16 [32, 1024, 384], P('expert', 'dp')
- grad_down_w: bfloat16 [32, 384, 1024], P('expert', 'dp')
The draws below stay inside these ranges and needn't reach their ends.
Inputs may be any that keep to these rules, and one draw needn't show every extreme that they name: `routing`: each row names 2 different experts; among the 128 rows of one device no expert is named by more than 16 rows.
All inputs are finite; a program needn't handle non-finite values.
Results may differ from the reference program's by a relative error of at most 0.018.
Values may be sent and summed in bfloat16 or wider, within the bound.
A program may use at most 64 MiB of HBM per device.

```python
import math
import jax
import jax.numpy as jnp
import numpy as np
from jax import lax

D = 1024
FF = 384
TOP = 2
TOK_DEV = 128
EXPERTS = 32
CAP = 16
GROUPS = 16
TOKENS = 65536
N_EXPERT = 32
DEVICES = 512


def place_ends(values, key, low, top_value):
    longest = values.shape.index(max(values.shape))
    spots = []
    for shift in (0, 1):
        where = [jax.random.randint(jax.random.fold_in(key, axis), (), 0, length) for axis, length in enumerate(values.shape)]
        where[longest] = (where[longest] + shift) % values.shape[longest]
        spots.append(tuple(where))
    return values.at[spots[0]].set(low).at[spots[1]].set(top_value)


def block_scale(stream_key, dims, split, low, high):
    factor_of = 1.0
    for position, blocks in split:
        heights = jax.random.uniform(jax.random.fold_in(jax.random.fold_in(stream_key, 6), position), (blocks,), jnp.float32, low / len(split), high / len(split))
        factor_of = factor_of * jnp.repeat(jnp.exp(heights), dims[position] // blocks).reshape((-1,) + (1,) * (len(dims) - 1 - position))
    return factor_of


def routed_block(own_key, own, number, rows, count, top, bound, lean):
    sequence = jax.random.permutation(own_key, count)
    crowded, usual = load_shares(count, rows * top, bound, lean, True), load_shares(count, rows * top, bound, lean, False)
    places = jnp.arange(count)

    def named(lengths, turn):
        used = int((lengths > 0).sum())
        fixed = max(1, used // 4)
        moved = fixed + (places - fixed + turn * (used - fixed)) % max(1, count - fixed)
        return jnp.zeros((count,), jnp.int32).at[sequence[jnp.where(places < fixed, places, moved)]].set(jnp.asarray(lengths, jnp.int32))

    lengths = jnp.where(number % 4 == 0, named(crowded, number // 4), named(usual, number - number // 4 - 1))
    mixed = jax.random.permutation(jax.random.fold_in(own, 3), count)
    donor, taker = mixed[0:count // 2 * 2:2], mixed[1:count // 2 * 2:2]
    room = jnp.minimum(lengths[donor] - 1, bound - lengths[taker]) // 2
    room = jnp.where((donor == sequence[0]) | (taker == sequence[0]) | (lengths[taker] == 0), 0, jnp.maximum(room, 0))
    moved = jax.random.randint(jax.random.fold_in(own, 4), (count // 2,), 0, 1 << 20) % (room + 1)
    lengths = lengths.at[donor].add(-moved).at[taker].add(moved)
    labels = jnp.searchsorted(jnp.cumsum(lengths), jnp.arange(rows * top), side="right").astype(jnp.int32)
    table = labels.reshape(top, rows).T
    table = table[jax.random.permutation(jax.random.fold_in(own, 1), rows)]
    turn = jax.random.randint(jax.random.fold_in(own, 2), (rows, 1), 0, top)
    return jnp.take_along_axis(table, (jnp.arange(top)[None, :] + turn) % top, axis=1)


def load_shares(count, total, limit, skew, full):
    weights = [(1 << 20) // math.isqrt(rank ** skew) + 1 for rank in range(1, count + 1)]
    largest = limit if full else min(limit, max(-(-total // count), total * weights[0] // sum(weights)))
    least = 1 if total - largest >= count - 1 else 0
    given, spare = [largest] + [least] * (count - 1), total - largest - least * (count - 1)
    while spare > 0:
        candidates = [i for i in range(1, count) if given[i] < largest] or [i for i in range(1, count) if given[i] < limit]
        whole, left = sum([weights[i] for i in candidates]), spare
        for i in candidates:
            more = min(limit - given[i], max(1, left * weights[i] // whole), spare)
            given[i] = given[i] + more
            spare = spare - more
    return np.array(given)


def scatter_about(rng, dims, deviation, reach, cuts=(), kind=jnp.bfloat16):
    gain = block_scale(rng, dims, cuts, -0.22, 0.18) if cuts else 1.0
    values = jax.random.normal(rng, dims, jnp.float32) * deviation * gain
    return jnp.minimum(jnp.maximum(values, -reach), reach).astype(kind)


def setup_inputs(seed: int = 0) -> dict:
    seeds = jax.random.split(jax.random.key(seed), 9)
    tokens = scatter_about(seeds[0], (TOKENS, D), 1.0, 6.0, ((0, 512),))
    cotangent = scatter_about(seeds[1], (TOKENS, D), 1.0, 6.0, ((0, 512),))
    routing_keys = jax.random.split(jax.random.fold_in(seeds[2], 1), TOKENS // TOK_DEV)
    routing_turns = jax.random.permutation(jax.random.fold_in(seeds[2], 3), TOKENS // TOK_DEV)
    routing = jax.vmap(lambda own, number: routed_block(jax.random.fold_in(seeds[2], 2), own, number, TOK_DEV, EXPERTS, TOP, CAP, 2))(routing_keys, routing_turns).reshape((TOKENS, TOP))
    gate_values = jnp.clip(0.1 + 0.9 * jax.random.uniform(seeds[3], (TOKENS, TOP), jnp.float32) ** block_scale(seeds[3], (TOKENS, TOP), ((0, 512),), -0.2, 0.2), 0.1, 1.0)
    live_counts = place_ends(jax.random.randint(seeds[4], (DEVICES,), TOK_DEV // 2, TOK_DEV + 1), jax.random.fold_in(seeds[4], 1), TOK_DEV // 2, TOK_DEV).astype(jnp.int32)
    gate_weights = scatter_about(seeds[5], (EXPERTS, D, FF), D ** -0.5, 0.1875, ((0, 32), (1, 16)))
    up_weights = scatter_about(seeds[6], (EXPERTS, D, FF), D ** -0.5, 0.1875, ((0, 32), (1, 16)))
    down_weights = scatter_about(seeds[7], (EXPERTS, FF, D), FF ** -0.5, 0.3125, ((0, 32), (1, 16)))
    return {"tokens": tokens, "cotangent": cotangent, "routing": routing, "gate_values": gate_values, "live_counts": live_counts, "gate_weights": gate_weights, "up_weights": up_weights, "down_weights": down_weights}


def contract_last(left, right):
    return lax.dot_general(left, right, (((1,), (1,)), ((), ())), preferred_element_type=jnp.float32)


def contract_first(left, right):
    return lax.dot_general(left, right, (((0,), (0,)), ((), ())), preferred_element_type=jnp.float32)


def expert_rows(rows_in, grads_in, gate_w, up_w, down_w):
    pre_gate = jnp.dot(rows_in, gate_w, preferred_element_type=jnp.float32)
    pre_up = jnp.dot(rows_in, up_w, preferred_element_type=jnp.float32)
    sigmoid_gate = jax.nn.sigmoid(pre_gate)
    swish_gate = pre_gate * sigmoid_gate
    hidden = (swish_gate * pre_up).astype(jnp.bfloat16)
    outputs = jnp.dot(hidden, down_w, preferred_element_type=jnp.float32).astype(jnp.bfloat16)
    hidden_grad = contract_last(grads_in, down_w)
    gate_pre = (hidden_grad * pre_up * sigmoid_gate * (1.0 + pre_gate * (1.0 - sigmoid_gate))).astype(jnp.bfloat16)
    up_pre = (hidden_grad * swish_gate).astype(jnp.bfloat16)
    token_part = (contract_last(gate_pre, gate_w) + contract_last(up_pre, up_w)).astype(jnp.bfloat16)
    return outputs, token_part, (contract_first(rows_in, gate_pre), contract_first(rows_in, up_pre), contract_first(hidden, grads_in))


def reference(tokens, cotangent, routing, gate_values, live_counts, gate_weights, up_weights, down_weights):
    group_tok = TOK_DEV * N_EXPERT
    rows_cap = 2 * TOK_DEV * TOP
    assigned = group_tok * TOP

    def one_group(state_now, group_idx):
        row_start = group_idx * group_tok
        group_tokens = lax.dynamic_slice_in_dim(tokens, row_start, group_tok, 0)
        group_cot = lax.dynamic_slice_in_dim(cotangent, row_start, group_tok, 0)
        group_routes = lax.dynamic_slice_in_dim(routing, row_start, group_tok, 0)
        group_gates = lax.dynamic_slice_in_dim(gate_values, row_start, group_tok, 0)
        counts = lax.dynamic_slice_in_dim(live_counts, (group_idx * N_EXPERT).astype(jnp.int32), N_EXPERT, 0)
        within = jnp.arange(group_tok, dtype=jnp.int32) % TOK_DEV
        alive_rows = within < jnp.repeat(counts, TOK_DEV)
        alive_flat = jnp.repeat(alive_rows, TOP)
        target = jnp.where(alive_flat, group_routes.reshape(-1), EXPERTS).astype(jnp.int32)
        pack_order = jnp.argsort(target, stable=True).astype(jnp.int32)
        per_expert = jnp.sum((target[:, None] == jnp.arange(EXPERTS, dtype=jnp.int32)[None, :]).astype(jnp.int32), axis=0)
        starts = jnp.cumsum(per_expert) - per_expert
        tokens_pad = jnp.concatenate([group_tokens, jnp.zeros((1, D), group_tokens.dtype)], 0)
        cot_pad = jnp.concatenate([group_cot, jnp.zeros((1, D), group_cot.dtype)], 0)
        gates_pad = jnp.concatenate([group_gates.reshape(-1), jnp.zeros((1,), jnp.float32)], 0)

        def one_expert(expert_idx):
            offsets = jnp.arange(rows_cap, dtype=jnp.int32)
            valid = offsets < per_expert[expert_idx]
            picked = jnp.clip(starts[expert_idx] + offsets, 0, assigned - 1).astype(jnp.int32)
            chosen = jnp.where(valid, pack_order[picked], assigned).astype(jnp.int32)
            token_of = (chosen // TOP).astype(jnp.int32)
            rows_in = tokens_pad[token_of]
            grads_in = (gates_pad[chosen][:, None] * cot_pad[token_of].astype(jnp.float32)).astype(jnp.bfloat16)
            outputs, token_part, grads = expert_rows(rows_in, grads_in, gate_weights[expert_idx], up_weights[expert_idx], down_weights[expert_idx])
            return outputs, token_part, grads, chosen

        outputs, parts, grads, chosen = lax.map(one_expert, jnp.arange(EXPERTS, dtype=jnp.int32))
        flat_chosen = chosen.reshape(-1)
        out_assign = jnp.zeros((assigned + 1, D), outputs.dtype).at[flat_chosen].set(outputs.reshape(-1, D))[:assigned]
        part_assign = jnp.zeros((assigned + 1, D), parts.dtype).at[flat_chosen].set(parts.reshape(-1, D))[:assigned]
        expert_out = out_assign.reshape(group_tok, TOP, D).astype(jnp.float32)
        mixed = jnp.sum(group_gates[:, :, None] * expert_out, axis=1).astype(jnp.bfloat16)
        gate_grad = jnp.einsum("td,tkd->tk", group_cot.astype(jnp.float32), expert_out)
        token_grad = jnp.sum(part_assign.reshape(group_tok, TOP, D).astype(jnp.float32), axis=1).astype(jnp.bfloat16)
        rounded = tuple(lax.optimization_barrier(piece.astype(jnp.bfloat16)).astype(jnp.float32) for piece in grads)
        state_next = tuple(first + second for first, second in zip(state_now, rounded))
        return state_next, (mixed, token_grad, gate_grad)

    initial = (jnp.zeros((EXPERTS, D, FF), jnp.float32), jnp.zeros((EXPERTS, D, FF), jnp.float32), jnp.zeros((EXPERTS, FF, D), jnp.float32))
    totals, stacked = lax.scan(one_group, initial, jnp.arange(GROUPS, dtype=jnp.int32))
    mixed = stacked[0].reshape(TOKENS, D)
    token_grad = stacked[1].reshape(TOKENS, D)
    gate_grad = stacked[2].reshape(TOKENS, TOP)
    grad_gate_w = (totals[0] / GROUPS).astype(jnp.bfloat16)
    grad_up_w = (totals[1] / GROUPS).astype(jnp.bfloat16)
    grad_down_w = (totals[2] / GROUPS).astype(jnp.bfloat16)
    return (mixed, token_grad, gate_grad, grad_gate_w, grad_up_w, grad_down_w)
```

```python
import functools

import jax
import jax.numpy as jnp
from jax import lax
from jax.experimental import pallas as pl
from jax.experimental.pallas import tpu as pltpu
from jax.sharding import PartitionSpec as P

NX, NY, NZL = 4, 4, 8
CAP = 16
BF, F32 = jnp.bfloat16, jnp.float32


def contract_last(left, right):
    return lax.dot_general(
        left, right, (((1,), (1,)), ((), ())), preferred_element_type=F32
    )


def contract_first(left, right):
    return lax.dot_general(
        left, right, (((0,), (0,)), ((), ())), preferred_element_type=F32
    )


def dot(left, right):
    return jnp.dot(left, right, preferred_element_type=F32)


def kernel(
    tok, cot, routing, gates, live,
    gate_in, up_in, down_in,
    mixed, token_grad, gate_grad, out_g, out_u, out_d,
    wg, wu, wd, down_full,
    send_x, send_c, recv_x, recv_c,
    send_o, send_p, back_o, back_p,
    hidden, pre_grads,
    own_g, own_u, own_d, sum_g, sum_u, sum_d, fin_g, fin_u, fin_d, land_g, land_u, land_d,
    ag_send, ag_recv, push_send, push_recv,
    rs_send, rs_recv, fin_send, fin_recv,
    a2a_send, a2a_recv, back_send, back_recv,
):
    rows_tok, width = tok.shape
    planes = 2 * NX * NY
    nz = 2 * NZL
    slots = planes * CAP
    ff = gate_in.shape[-1]

    dp, ex = lax.axis_index("dp"), lax.axis_index("expert")
    zl, c = lax.div(dp, 2), lax.rem(dp, 2)
    y, zh, x = lax.div(ex, 2 * NX), lax.rem(lax.div(ex, NX), 2), lax.rem(ex, NX)
    z = zh * NZL + zl
    me = y * (2 * NX) + c * NX + x

    def along_z(zz, core):
        return (lax.rem(zz, NZL) * 2 + core, y * (2 * NX) + lax.div(zz, NZL) * NX + x)

    def in_plane(q):
        qy, qc, qx = lax.div(q, 2 * NX), lax.rem(lax.div(q, NX), 2), lax.rem(q, NX)
        return (zl * 2 + qc, qy * (2 * NX) + zh * NX + qx)

    ring = (along_z(lax.rem(z + 1, nz), c), along_z(lax.rem(z + nz - 1, nz), c))
    other = along_z(z, 1 - c)
    reach = (NZL, NZL - 1)

    def remote(src, dst, send_sem, recv_sem, device):
        return pltpu.make_async_remote_copy(
            src_ref=src, dst_ref=dst, send_sem=send_sem, recv_sem=recv_sem,
            device_id=device, device_id_type=pl.DeviceIdType.MESH,
        )

    barrier = pltpu.get_barrier_semaphore()

    def greet(o, _):
        pl.semaphore_signal(
            barrier, inc=1, device_id=in_plane(lax.rem(me + o, planes)),
            device_id_type=pl.DeviceIdType.MESH,
        )
        return 0

    for device in ring:
        pl.semaphore_signal(
            barrier, inc=1, device_id=device, device_id_type=pl.DeviceIdType.MESH
        )
    lax.fori_loop(1, planes, greet, 0)
    pl.semaphore_wait(barrier, planes + 1)

    shards_in = (gate_in, up_in, down_in)
    weights = (wg, wu, wd)

    def push(q):
        return remote(
            shards_in[q].at[0], weights[q].at[dp], push_send.at[q], push_recv.at[q], other
        )

    def ag_copy(q, flow, block):
        at = weights[q].at[pl.ds(2 * block, 2)]
        return remote(at, at, ag_send.at[flow, block, q], ag_recv.at[block, q], ring[flow])

    def source(flow, hops):
        zz = lax.rem(z - hops + nz, nz) if flow == 0 else lax.rem(z + hops, nz)
        return lax.rem(zz, NZL), lax.div(zz, NZL) == c

    @pl.when(zh != c)
    def _():
        for q in range(3):
            push(q).start()

    @pl.when(zh == c)
    def _():
        for q in range(3):
            weights[q][dp] = shards_in[q][0]
        for q in range(3):
            pltpu.make_async_copy(weights[q].at[dp], weights[q].at[dp], push_recv.at[q]).wait()
            for flow in (0, 1):
                ag_copy(q, flow, zl).start()

    eye = lax.broadcasted_iota(jnp.int32, (rows_tok, rows_tok), 0) == lax.broadcasted_iota(
        jnp.int32, (rows_tok, rows_tok), 1
    )

    def column(row):
        return jnp.sum(jnp.where(eye, row, 0.0), axis=1, keepdims=True)

    def row_of(col):
        return jnp.sum(jnp.where(eye, col, 0.0), axis=0, keepdims=True)

    alive = lax.broadcasted_iota(jnp.int32, (rows_tok, 1), 0) < live[0]
    lanes = lax.broadcasted_iota(jnp.int32, (rows_tok, planes), 1).astype(F32)
    earlier = (
        lax.broadcasted_iota(jnp.int32, (rows_tok, rows_tok), 1)
        < lax.broadcasted_iota(jnp.int32, (rows_tok, rows_tok), 0)
    ).astype(BF)
    slot, weight = [], []
    taken = jnp.zeros((1, planes), F32)
    for k in range(2):
        expert = column(routing[k : k + 1, :].astype(F32))
        weight.append(column(gates[k : k + 1, :]))
        onehot = jnp.where((expert == lanes) & alive, 1.0, 0.0)
        before = dot(earlier, onehot.astype(BF)) + taken
        taken = taken + jnp.sum(onehot, axis=0, keepdims=True)
        found = jnp.sum(onehot * (before + lanes * CAP), axis=1, keepdims=True)
        slot.append(jnp.where(alive, found, -1.0).astype(jnp.int32))

    def picks(k, start, count):
        at = lax.broadcasted_iota(jnp.int32, (rows_tok, count), 1) + start
        return jnp.where(slot[k] == at, 1.0, 0.0).astype(BF)

    scaled = [(weight[k] * cot[...].astype(F32)).astype(BF) for k in range(2)]

    def dispatch(q):
        return (
            remote(send_x.at[q], recv_x.at[me], a2a_send.at[0], a2a_recv.at[0], in_plane(q)),
            remote(send_c.at[q], recv_c.at[me], a2a_send.at[1], a2a_recv.at[1], in_plane(q)),
        )

    group = 2 * NX
    for j in range(NY):
        first = lax.rem(y + j, NY) * group
        p0, p1 = (picks(k, first * CAP, group * CAP) for k in range(2))
        shape = (group, CAP, width)
        send_x[pl.ds(first, group)] = contract_first(p0 + p1, tok[...]).astype(BF).reshape(shape)
        send_c[pl.ds(first, group)] = (
            (contract_first(p0, scaled[0]) + contract_first(p1, scaled[1])).astype(BF).reshape(shape)
        )

        def send(o, _, first=first):
            q = first + lax.rem(x + o, group)

            @pl.when(q != me)
            def _():
                for copy in dispatch(q):
                    copy.start()

            return 0

        lax.fori_loop(0, group, send, 0)
    recv_x[me] = send_x[me]
    recv_c[me] = send_c[me]

    def forward(s, _):
        for q in range(3):
            for flow in (0, 1):
                block, ours = source(flow, s)

                @pl.when(ours & (s <= reach[flow]))
                def _(q=q, flow=flow, block=block):
                    ag_copy(q, flow, block).wait_recv()

                    @pl.when(s < reach[flow])
                    def _():
                        ag_copy(q, flow, block).start()

        return 0

    lax.fori_loop(1, NZL + 1, forward, 0)

    shard_rows = down_in.shape[1]
    for i in range(nz):
        down_full[i * shard_rows : (i + 1) * shard_rows] = wd[i]

    def all_of(ref, sem, count):
        part = ref.at[pl.ds(0, count)]
        pltpu.make_async_copy(part, part, sem).wait()

    all_of(recv_x, a2a_recv.at[0], planes - 1)
    all_of(recv_c, a2a_recv.at[1], planes - 1)

    tiles = 2
    per = planes // tiles
    tile_rows = per * CAP

    def combine(q):
        return (
            remote(send_o.at[q], back_o.at[me], back_send.at[0], back_recv.at[0], in_plane(q)),
            remote(send_p.at[q], back_p.at[me], back_send.at[1], back_recv.at[1], in_plane(q)),
        )

    def tile(t, _):
        first = lax.rem(lax.div(y * tiles, NY) + t, tiles) * per
        rows = pl.multiple_of(first * CAP, tile_rows)
        xs = recv_x[pl.ds(first, per)].reshape(tile_rows, width)
        cs = recv_c[pl.ds(first, per)].reshape(tile_rows, width)
        gate_w = wg[...].reshape(width, ff)
        up_w = wu[...].reshape(width, ff)
        down_w = down_full[...]
        pre_gate = dot(xs, gate_w)
        pre_up = dot(xs, up_w)
        sig = jax.nn.sigmoid(pre_gate)
        swish = pre_gate * sig
        hid = (swish * pre_up).astype(BF)
        hidden[pl.ds(rows, tile_rows)] = hid
        send_o[pl.ds(first, per)] = dot(hid, down_w).astype(BF).reshape(per, CAP, width)
        hidden_grad = contract_last(cs, down_w)
        gate_pre = (hidden_grad * pre_up * sig * (1.0 + pre_gate * (1.0 - sig))).astype(BF)
        up_pre = (hidden_grad * swish).astype(BF)
        pre_grads[pl.ds(rows, tile_rows), :ff] = gate_pre
        pre_grads[pl.ds(rows, tile_rows), ff:] = up_pre
        part = contract_last(gate_pre, gate_w) + contract_last(up_pre, up_w)
        send_p[pl.ds(first, per)] = part.astype(BF).reshape(per, CAP, width)

        def send(o, _):
            q = first + lax.rem(group * (y % 2) + x + o, per)

            @pl.when(q != me)
            def _():
                for copy in combine(q):
                    copy.start()

            return 0

        lax.fori_loop(0, per, send, 0)
        return 0

    lax.fori_loop(0, tiles, tile, 0)
    back_o[me] = send_o[me]
    back_p[me] = send_p[me]

    own, sums = (own_g, own_u, own_d), (sum_g, sum_u, sum_d)
    both = contract_first(recv_x[...].reshape(slots, width), pre_grads[...])
    own_g[...] = both[:, :ff].astype(BF).reshape(own_g.shape)
    own_u[...] = both[:, ff:].astype(BF).reshape(own_u.shape)
    down_grad = contract_first(hidden[...], recv_c[...].reshape(slots, width))
    for i in range(nz):
        own_d[i] = down_grad[i * shard_rows : (i + 1) * shard_rows].astype(BF)

    def rs_copy(q, flow, block, src):
        at = sums[q].at[flow, pl.ds(2 * block, 2)]
        return remote(src, at, rs_send.at[flow, block, q], rs_recv.at[flow, block, q], ring[flow])

    def target(flow, hops):
        return source(1 - flow, hops)

    def summing(s, _):
        for q in range(3):
            for flow in (0, 1):
                left = reach[flow] - s
                block, ours = target(flow, left)
                here = pl.ds(2 * block, 2)

                @pl.when(ours & (left > 0))
                def _(q=q, flow=flow, block=block, here=here):
                    @pl.when(s == 0)
                    def _():
                        rs_copy(q, flow, block, own[q].at[here]).start()

                    @pl.when(s > 0)
                    def _():
                        at = sums[q].at[flow, here]
                        rs_copy(q, flow, block, at).wait_recv()
                        sums[q][flow, here] = (
                            sums[q][flow, here].astype(F32) + own[q][here].astype(F32)
                        ).astype(BF)
                        rs_copy(q, flow, block, at).start()

        return 0

    lax.fori_loop(0, NZL, summing, 0)

    all_of(back_o, back_recv.at[0], planes - 1)
    all_of(back_p, back_recv.at[1], planes - 1)
    p0, p1 = (picks(k, 0, slots) for k in range(2))
    token_grad[...] = dot(p0 + p1, back_p[...].reshape(slots, width)).astype(BF)
    total = jnp.zeros((rows_tok, width), F32)
    cot_f = cot[...].astype(F32)
    for k, p in enumerate((p0, p1)):
        got = dot(p, back_o[...].reshape(slots, width))
        total += weight[k] * got
        gate_grad[k : k + 1, :] = row_of(jnp.sum(cot_f * got, axis=1, keepdims=True))
    mixed[...] = total.astype(BF)

    outs, fins, lands = (out_g, out_u, out_d), (fin_g, fin_u, fin_d), (land_g, land_u, land_d)

    def fin_copy(q):
        return remote(fins[q].at[1 - c], lands[q], fin_send.at[q], fin_recv.at[q], other)

    @pl.when(zh == c)
    def _():
        here = pl.ds(2 * zl, 2)
        for q in range(3):
            for flow in (0, 1):
                at = sums[q].at[flow, here]
                rs_copy(q, flow, zl, at).wait_recv()
            fins[q][...] = (
                (
                    own[q][here].astype(F32)
                    + sums[q][0, here].astype(F32)
                    + sums[q][1, here].astype(F32)
                )
                * (1.0 / nz)
            ).astype(BF)
            fin_copy(q).start()
            outs[q][0] = fins[q][c]
        for q in range(3):
            fin_copy(q).wait_send()

    @pl.when(zh != c)
    def _():
        for q in range(3):
            fin_copy(q).wait_recv()
            outs[q][0] = lands[q][...]

    @pl.when(zh != c)
    def _():
        for q in range(3):
            push(q).wait_send()

    def sent(s, _):
        for q in range(3):
            for flow in (0, 1):
                block, ours = source(flow, s)

                @pl.when(ours & (s < reach[flow]))
                def _(q=q, flow=flow, block=block):
                    ag_copy(q, flow, block).wait_send()

                block, ours = target(flow, s + 1)

                @pl.when(ours & (s < reach[flow]))
                def _(q=q, flow=flow, block=block):
                    rs_copy(q, flow, block, own[q].at[pl.ds(2 * block, 2)]).wait_send()

        return 0

    lax.fori_loop(0, NZL, sent, 0)
    for ref, sem in (
        (send_x, a2a_send.at[0]),
        (send_c, a2a_send.at[1]),
        (send_o, back_send.at[0]),
        (send_p, back_send.at[1]),
    ):
        all_of(ref, sem, planes - 1)


def shards(
    tokens, cotangent, routing, gate_values, live_counts, gate_weights, up_weights, down_weights
):
    rows_tok, width = tokens.shape
    ff = gate_weights.shape[-1]
    planes, nz = 2 * NX * NY, 2 * NZL
    slots = planes * CAP
    shapes = [gate_weights.shape[1:], up_weights.shape[1:], down_weights.shape[1:]]
    vmem = pl.BlockSpec(memory_space=pltpu.VMEM)
    dma = pltpu.SemaphoreType.DMA
    block = pltpu.VMEM((planes, CAP, width), BF)
    flops = 18 * slots * width * ff
    outs = pl.pallas_call(
        kernel,
        out_shape=(
            jax.ShapeDtypeStruct((rows_tok, width), BF),
            jax.ShapeDtypeStruct((rows_tok, width), BF),
            jax.ShapeDtypeStruct((2, rows_tok), F32),
            *(jax.ShapeDtypeStruct((1, *s), BF) for s in shapes),
        ),
        in_specs=[vmem] * 4 + [pl.BlockSpec(memory_space=pltpu.SMEM)] + [vmem] * 3,
        out_specs=tuple([vmem] * 6),
        scratch_shapes=[
            *(pltpu.VMEM((nz, *s), BF) for s in shapes),
            pltpu.VMEM((ff, width), BF),
            *([block] * 8),
            pltpu.VMEM((slots, ff), BF),
            pltpu.VMEM((slots, 2 * ff), BF),
            *(pltpu.VMEM((nz, *s), BF) for s in shapes),
            *(pltpu.VMEM((2, nz, *s), BF) for s in shapes),
            *(pltpu.VMEM((2, *s), BF) for s in shapes),
            *(pltpu.VMEM(s, BF) for s in shapes),
            dma((2, NZL, 3)),
            dma((NZL, 3)),
            dma((3,)),
            dma((3,)),
            dma((2, NZL, 3)),
            dma((2, NZL, 3)),
            dma((3,)),
            dma((3,)),
            dma((2,)),
            dma((2,)),
            dma((2,)),
            dma((2,)),
        ],
        compiler_params=pltpu.CompilerParams(
            collective_id=0, has_side_effects=True, vmem_limit_bytes=56 * 1024 * 1024
        ),
        cost_estimate=pl.CostEstimate(
            flops=flops, bytes_accessed=2 * 1024 * 1024, transcendentals=slots * ff
        ),
    )(
        tokens, cotangent, routing.T, gate_values.T, live_counts,
        gate_weights, up_weights, down_weights,
    )
    mixed, token_grad, gate_grad, grad_g, grad_u, grad_d = outs
    return mixed, token_grad, gate_grad.T, grad_g, grad_u, grad_d


def solution(mesh):
    return jax.shard_map(
        shards,
        mesh=mesh,
        in_specs=(
            P(("dp", "expert"), None),
            P(("dp", "expert"), None),
            P(("dp", "expert"), None),
            P(("dp", "expert"), None),
            P(("dp", "expert")),
            P("expert", "dp", None),
            P("expert", "dp", None),
            P("expert", "dp", None),
        ),
        out_specs=(
            P(("dp", "expert"), None),
            P(("dp", "expert"), None),
            P(("dp", "expert"), None),
            P("expert", "dp", None),
            P("expert", "dp", None),
            P("expert", "dp", None),
        ),
        check_vma=False,
    )
```

```python
import functools

import jax
import jax.numpy as jnp
from jax import lax
from jax.experimental import pallas as pl
from jax.experimental.pallas import tpu as pltpu
from jax.sharding import PartitionSpec as P

NX, NY, NZL = 4, 4, 8
CAP = 16
BF, F32 = jnp.bfloat16, jnp.float32


def contract_last(left, right):
    return lax.dot_general(
        left, right, (((1,), (1,)), ((), ())), preferred_element_type=F32
    )


def contract_first(left, right):
    return lax.dot_general(
        left, right, (((0,), (0,)), ((), ())), preferred_element_type=F32
    )


def dot(left, right):
    return jnp.dot(left, right, preferred_element_type=F32)


def kernel(
    tok, cot, routing, gates, live,
    gate_in, up_in, down_in,
    mixed, token_grad, gate_grad, out_g, out_u, out_d,
    wg, wu, wd, down_full,
    send_x, send_c, recv_x, recv_c,
    send_o, send_p, back_o, back_p,
    hidden, pre_grads,
    own_g, own_u, own_d, sum_g, sum_u, sum_d, fin_g, fin_u, fin_d, land_g, land_u, land_d,
    ag_send, ag_recv, push_send, push_recv,
    rs_send, rs_recv, fin_send, fin_recv,
    a2a_send, a2a_recv, back_send, back_recv,
):
    rows_tok, width = tok.shape
    planes = 2 * NX * NY
    nz = 2 * NZL
    slots = planes * CAP
    ff = gate_in.shape[-1]

    dp, ex = lax.axis_index("dp"), lax.axis_index("expert")
    zl, c = lax.div(dp, 2), lax.rem(dp, 2)
    y, zh, x = lax.div(ex, 2 * NX), lax.rem(lax.div(ex, NX), 2), lax.rem(ex, NX)
    z = zh * NZL + zl
    half = NX * NY
    spot = y * NX + x
    me = c * half + spot

    def along_z(zz, core):
        return (lax.rem(zz, NZL) * 2 + core, y * (2 * NX) + lax.div(zz, NZL) * NX + x)

    def in_plane(q):
        qc, qy, qx = lax.div(q, half), lax.rem(lax.div(q, NX), NY), lax.rem(q, NX)
        return (zl * 2 + qc, qy * (2 * NX) + zh * NX + qx)

    ring = (along_z(lax.rem(z + 1, nz), c), along_z(lax.rem(z + nz - 1, nz), c))
    other = along_z(z, 1 - c)

    def reach(flow, h):
        return NZL - lax.rem(h + flow, 2)

    def mixed_order(o):
        dx = lax.rem(o, NX)
        dy = lax.rem(lax.div(o, NX) + dx, NY)
        return lax.rem(y + dy, NY) * NX + lax.rem(x + dx, NX)

    def remote(src, dst, send_sem, recv_sem, device):
        return pltpu.make_async_remote_copy(
            src_ref=src, dst_ref=dst, send_sem=send_sem, recv_sem=recv_sem,
            device_id=device, device_id_type=pl.DeviceIdType.MESH,
        )

    barrier = pltpu.get_barrier_semaphore()

    def greet(o, _):
        pl.semaphore_signal(
            barrier, inc=1, device_id=in_plane(lax.rem(me + o, planes)),
            device_id_type=pl.DeviceIdType.MESH,
        )
        return 0

    for device in ring:
        pl.semaphore_signal(
            barrier, inc=1, device_id=device, device_id_type=pl.DeviceIdType.MESH
        )
    lax.fori_loop(1, planes, greet, 0)
    pl.semaphore_wait(barrier, planes + 1)

    shards_in = (gate_in, up_in, down_in)
    weights = (wg, wu, wd)

    def push(q):
        return remote(
            shards_in[q].at[0], weights[q].at[dp], push_send.at[q], push_recv.at[q], other
        )

    def ag_copy(q, flow, block, h):
        at = weights[q].at[2 * block + h]
        return remote(at, at, ag_send.at[flow, block, h, q], ag_recv.at[block, h, q], ring[flow])

    def source(flow, hops):
        zz = lax.rem(z - hops + nz, nz) if flow == 0 else lax.rem(z + hops, nz)
        return lax.rem(zz, NZL), lax.div(zz, NZL) == c

    @pl.when(zh != c)
    def _():
        for q in range(3):
            push(q).start()

    @pl.when(zh == c)
    def _():
        for q in range(3):
            weights[q][dp] = shards_in[q][0]
            for flow in (0, 1):
                ag_copy(q, flow, zl, c).start()
        for q in range(3):
            pltpu.make_async_copy(weights[q].at[dp], weights[q].at[dp], push_recv.at[q]).wait()
            for flow in (0, 1):
                ag_copy(q, flow, zl, 1 - c).start()

    eye = lax.broadcasted_iota(jnp.int32, (rows_tok, rows_tok), 0) == lax.broadcasted_iota(
        jnp.int32, (rows_tok, rows_tok), 1
    )

    def column(row):
        return jnp.sum(jnp.where(eye, row, 0.0), axis=1, keepdims=True)

    def row_of(col):
        return jnp.sum(jnp.where(eye, col, 0.0), axis=0, keepdims=True)

    alive = lax.broadcasted_iota(jnp.int32, (rows_tok, 1), 0) < live[0]
    lanes = lax.broadcasted_iota(jnp.int32, (rows_tok, planes), 1).astype(F32)
    earlier = (
        lax.broadcasted_iota(jnp.int32, (rows_tok, rows_tok), 1)
        < lax.broadcasted_iota(jnp.int32, (rows_tok, rows_tok), 0)
    ).astype(BF)
    slot, weight = [], []
    taken = jnp.zeros((1, planes), F32)
    for k in range(2):
        named = routing[k : k + 1, :]
        qy, qc, qx = lax.div(named, 2 * NX), lax.rem(lax.div(named, NX), 2), lax.rem(named, NX)
        expert = column((qc * half + qy * NX + qx).astype(F32))
        weight.append(column(gates[k : k + 1, :]))
        onehot = jnp.where((expert == lanes) & alive, 1.0, 0.0)
        before = dot(earlier, onehot.astype(BF)) + taken
        taken = taken + jnp.sum(onehot, axis=0, keepdims=True)
        found = jnp.sum(onehot * (before + lanes * CAP), axis=1, keepdims=True)
        slot.append(jnp.where(alive, found, -1.0).astype(jnp.int32))

    def picks(k, start, count):
        at = lax.broadcasted_iota(jnp.int32, (rows_tok, count), 1) + start
        return jnp.where(slot[k] == at, 1.0, 0.0).astype(BF)

    scaled = [(weight[k] * cot[...].astype(F32)).astype(BF) for k in range(2)]

    def dispatch(q):
        return (
            remote(send_x.at[q], recv_x.at[me], a2a_send.at[0], a2a_recv.at[0], in_plane(q)),
            remote(send_c.at[q], recv_c.at[me], a2a_send.at[1], a2a_recv.at[1], in_plane(q)),
        )

    for j in range(2):
        first = lax.rem(c + j, 2) * half
        p0, p1 = (picks(k, first * CAP, half * CAP) for k in range(2))
        shape = (half, CAP, width)
        send_x[pl.ds(first, half)] = contract_first(p0 + p1, tok[...]).astype(BF).reshape(shape)
        send_c[pl.ds(first, half)] = (
            (contract_first(p0, scaled[0]) + contract_first(p1, scaled[1])).astype(BF).reshape(shape)
        )

        def send(o, _, first=first):
            q = first + mixed_order(o)

            @pl.when(q != me)
            def _():
                for copy in dispatch(q):
                    copy.start()

            return 0

        lax.fori_loop(0, half, send, 0)
    recv_x[me] = send_x[me]
    recv_c[me] = send_c[me]

    def forward(s, _):
        for h in range(2):
            for q in range(3):
                for flow in (0, 1):
                    block, ours = source(flow, s)
                    far = reach(flow, h)

                    @pl.when(ours & (s <= far))
                    def _(q=q, flow=flow, h=h, block=block, far=far):
                        ag_copy(q, flow, block, h).wait_recv()

                        @pl.when(s < far)
                        def _():
                            ag_copy(q, flow, block, h).start()

        return 0

    lax.fori_loop(1, NZL + 1, forward, 0)

    shard_rows = down_in.shape[1]
    for i in range(nz):
        down_full[i * shard_rows : (i + 1) * shard_rows] = wd[i]

    def all_of(ref, sem, count):
        part = ref.at[pl.ds(0, count)]
        pltpu.make_async_copy(part, part, sem).wait()

    all_of(recv_x, a2a_recv.at[0], planes - 1)
    all_of(recv_c, a2a_recv.at[1], planes - 1)

    tiles = 2
    per = planes // tiles
    tile_rows = per * CAP

    def gate_up():
        return wg[...].reshape(width, ff), wu[...].reshape(width, ff)

    def inner(t, _):
        first = t * per
        rows = pl.ds(pl.multiple_of(first * CAP, tile_rows), tile_rows)
        xs = recv_x[pl.ds(first, per)].reshape(tile_rows, width)
        cs = recv_c[pl.ds(first, per)].reshape(tile_rows, width)
        gate_w, up_w = gate_up()
        pre_gate = dot(xs, gate_w)
        pre_up = dot(xs, up_w)
        hidden_grad = contract_last(cs, down_full[...])
        sig = jax.nn.sigmoid(pre_gate)
        swish = pre_gate * sig
        hidden[rows] = (swish * pre_up).astype(BF)
        pre_grads[rows, :ff] = (
            hidden_grad * pre_up * sig * (1.0 + pre_gate * (1.0 - sig))
        ).astype(BF)
        pre_grads[rows, ff:] = (hidden_grad * swish).astype(BF)
        return 0

    lax.fori_loop(0, tiles, inner, 0)

    own, sums = (own_g, own_u, own_d), (sum_g, sum_u, sum_d)
    both = contract_first(recv_x[...].reshape(slots, width), pre_grads[...])
    own_g[...] = both[:, :ff].astype(BF).reshape(own_g.shape)
    own_u[...] = both[:, ff:].astype(BF).reshape(own_u.shape)
    down_grad = contract_first(hidden[...], recv_c[...].reshape(slots, width))
    for i in range(nz):
        own_d[i] = down_grad[i * shard_rows : (i + 1) * shard_rows].astype(BF)

    def rs_copy(q, flow, block, h, src):
        at = sums[q].at[flow, 2 * block + h]
        return remote(
            src, at, rs_send.at[flow, block, h, q], rs_recv.at[flow, block, h, q], ring[flow]
        )

    def target(flow, hops):
        return source(1 - flow, hops)

    for h in range(2):
        for q in range(3):
            for flow in (0, 1):
                block, ours = target(flow, reach(flow, h))

                @pl.when(ours)
                def _(q=q, flow=flow, h=h, block=block):
                    rs_copy(q, flow, block, h, own[q].at[2 * block + h]).start()

    def combine(q):
        return (
            remote(send_o.at[q], back_o.at[me], back_send.at[0], back_recv.at[0], in_plane(q)),
            remote(send_p.at[q], back_p.at[me], back_send.at[1], back_recv.at[1], in_plane(q)),
        )

    def outer(t, _):
        first = lax.rem(t + c, tiles) * per
        rows = pl.ds(pl.multiple_of(first * CAP, tile_rows), tile_rows)
        gate_w, up_w = gate_up()
        shape = (per, CAP, width)
        send_o[pl.ds(first, per)] = dot(hidden[rows], down_full[...]).astype(BF).reshape(shape)
        part = contract_last(pre_grads[rows, :ff], gate_w)
        part += contract_last(pre_grads[rows, ff:], up_w)
        send_p[pl.ds(first, per)] = part.astype(BF).reshape(shape)

        def send(o, _):
            q = first + mixed_order(o)

            @pl.when(q != me)
            def _():
                for copy in combine(q):
                    copy.start()

            return 0

        lax.fori_loop(0, per, send, 0)
        return 0

    lax.fori_loop(0, tiles, outer, 0)
    back_o[me] = send_o[me]
    back_p[me] = send_p[me]

    def summing(s, _):
        for h in range(2):
            for q in range(3):
                for flow in (0, 1):
                    left = reach(flow, h) - s
                    block, ours = target(flow, left)

                    @pl.when(ours & (left > 0))
                    def _(q=q, flow=flow, h=h, block=block):
                        here = 2 * block + h
                        at = sums[q].at[flow, here]
                        rs_copy(q, flow, block, h, at).wait_recv()
                        sums[q][flow, here] = (
                            sums[q][flow, here].astype(F32) + own[q][here].astype(F32)
                        ).astype(BF)
                        rs_copy(q, flow, block, h, at).start()

        return 0

    lax.fori_loop(1, NZL, summing, 0)

    all_of(back_o, back_recv.at[0], planes - 1)
    all_of(back_p, back_recv.at[1], planes - 1)
    p0, p1 = (picks(k, 0, slots) for k in range(2))
    token_grad[...] = dot(p0 + p1, back_p[...].reshape(slots, width)).astype(BF)
    total = jnp.zeros((rows_tok, width), F32)
    cot_f = cot[...].astype(F32)
    for k, p in enumerate((p0, p1)):
        got = dot(p, back_o[...].reshape(slots, width))
        total += weight[k] * got
        gate_grad[k : k + 1, :] = row_of(jnp.sum(cot_f * got, axis=1, keepdims=True))
    mixed[...] = total.astype(BF)

    outs, fins, lands = (out_g, out_u, out_d), (fin_g, fin_u, fin_d), (land_g, land_u, land_d)

    def fin_copy(q):
        return remote(fins[q].at[1 - c], lands[q], fin_send.at[q], fin_recv.at[q], other)

    @pl.when(zh == c)
    def _():
        for h in (1 - c, c):
            here = 2 * zl + h
            for q in range(3):
                for flow in (0, 1):
                    at = sums[q].at[flow, here]
                    rs_copy(q, flow, zl, h, at).wait_recv()
                fins[q][h] = (
                    (
                        own[q][here].astype(F32)
                        + sums[q][0, here].astype(F32)
                        + sums[q][1, here].astype(F32)
                    )
                    * (1.0 / nz)
                ).astype(BF)
                if h is not c:
                    fin_copy(q).start()
        for q in range(3):
            outs[q][0] = fins[q][c]
            fin_copy(q).wait_send()

    @pl.when(zh != c)
    def _():
        for q in range(3):
            fin_copy(q).wait_recv()
            outs[q][0] = lands[q][...]

    @pl.when(zh != c)
    def _():
        for q in range(3):
            push(q).wait_send()

    def sent(s, _):
        for h in range(2):
            for q in range(3):
                for flow in (0, 1):
                    far = reach(flow, h)
                    block, ours = source(flow, s)

                    @pl.when(ours & (s < far))
                    def _(q=q, flow=flow, h=h, block=block):
                        ag_copy(q, flow, block, h).wait_send()

                    block, ours = target(flow, s + 1)

                    @pl.when(ours & (s < far))
                    def _(q=q, flow=flow, h=h, block=block):
                        rs_copy(q, flow, block, h, own[q].at[2 * block + h]).wait_send()

        return 0

    lax.fori_loop(0, NZL, sent, 0)
    for ref, sem in (
        (send_x, a2a_send.at[0]),
        (send_c, a2a_send.at[1]),
        (send_o, back_send.at[0]),
        (send_p, back_send.at[1]),
    ):
        all_of(ref, sem, planes - 1)


def hand_over(*refs):
    half = len(refs) // 3
    copies = [
        pltpu.make_async_copy(refs[i], refs[half + i], refs[2 * half + i]) for i in range(half)
    ]
    for copy in copies:
        copy.start()
    for copy in copies:
        copy.wait()


def shards(
    tokens, cotangent, routing, gate_values, live_counts, gate_weights, up_weights, down_weights
):
    rows_tok, width = tokens.shape
    ff = gate_weights.shape[-1]
    planes, nz = 2 * NX * NY, 2 * NZL
    slots = planes * CAP
    shapes = [gate_weights.shape[1:], up_weights.shape[1:], down_weights.shape[1:]]
    vmem = pl.BlockSpec(memory_space=pltpu.VMEM)
    dma = pltpu.SemaphoreType.DMA
    block = pltpu.VMEM((planes, CAP, width), BF)
    flops = 18 * slots * width * ff
    outs = pl.pallas_call(
        kernel,
        out_shape=(
            jax.ShapeDtypeStruct((rows_tok, width), BF),
            jax.ShapeDtypeStruct((rows_tok, width), BF),
            jax.ShapeDtypeStruct((2, rows_tok), F32),
            *(jax.ShapeDtypeStruct((1, *s), BF) for s in shapes),
        ),
        in_specs=[vmem] * 4 + [pl.BlockSpec(memory_space=pltpu.SMEM)] + [vmem] * 3,
        out_specs=tuple([vmem] * 6),
        scratch_shapes=[
            *(pltpu.VMEM((nz, *s), BF) for s in shapes),
            pltpu.VMEM((ff, width), BF),
            *([block] * 8),
            pltpu.VMEM((slots, ff), BF),
            pltpu.VMEM((slots, 2 * ff), BF),
            *(pltpu.VMEM((nz, *s), BF) for s in shapes),
            *(pltpu.VMEM((2, nz, *s), BF) for s in shapes),
            *(pltpu.VMEM((2, *s), BF) for s in shapes),
            *(pltpu.VMEM(s, BF) for s in shapes),
            dma((2, NZL, 2, 3)),
            dma((NZL, 2, 3)),
            dma((3,)),
            dma((3,)),
            dma((2, NZL, 2, 3)),
            dma((2, NZL, 2, 3)),
            dma((3,)),
            dma((3,)),
            dma((2,)),
            dma((2,)),
            dma((2,)),
            dma((2,)),
        ],
        compiler_params=pltpu.CompilerParams(
            collective_id=0, has_side_effects=True, vmem_limit_bytes=56 * 1024 * 1024
        ),
        cost_estimate=pl.CostEstimate(
            flops=flops, bytes_accessed=2 * 1024 * 1024, transcendentals=slots * ff
        ),
    )(
        tokens, cotangent, routing.T, gate_values.T, live_counts,
        gate_weights, up_weights, down_weights,
    )
    hbm = pl.BlockSpec(memory_space=pl.ANY)
    outs = pl.pallas_call(
        hand_over,
        out_shape=tuple(jax.ShapeDtypeStruct(o.shape, o.dtype) for o in outs),
        in_specs=[hbm] * len(outs),
        out_specs=tuple([hbm] * len(outs)),
        scratch_shapes=[pltpu.SemaphoreType.DMA] * len(outs),
    )(*outs)
    mixed, token_grad, gate_grad, grad_g, grad_u, grad_d = outs
    return mixed, token_grad, gate_grad.T, grad_g, grad_u, grad_d


def solution(mesh):
    return jax.shard_map(
        shards,
        mesh=mesh,
        in_specs=(
            P(("dp", "expert"), None),
            P(("dp", "expert"), None),
            P(("dp", "expert"), None),
            P(("dp", "expert"), None),
            P(("dp", "expert")),
            P("expert", "dp", None),
            P("expert", "dp", None),
            P("expert", "dp", None),
        ),
        out_specs=(
            P(("dp", "expert"), None),
            P(("dp", "expert"), None),
            P(("dp", "expert"), None),
            P("expert", "dp", None),
            P("expert", "dp", None),
            P("expert", "dp", None),
        ),
        check_vma=False,
    )
```

```python
import functools

import jax
import jax.numpy as jnp
from jax import lax
from jax.experimental import pallas as pl
from jax.experimental.pallas import tpu as pltpu
from jax.sharding import PartitionSpec as P

NX, NY, NZL = 4, 4, 8
CAP = 16
BF, F32 = jnp.bfloat16, jnp.float32


def contract_last(left, right):
    return lax.dot_general(
        left, right, (((1,), (1,)), ((), ())), preferred_element_type=F32
    )


def contract_first(left, right):
    return lax.dot_general(
        left, right, (((0,), (0,)), ((), ())), preferred_element_type=F32
    )


def dot(left, right):
    return jnp.dot(left, right, preferred_element_type=F32)


def kernel(
    tok, cot, routing, gates, live,
    gate_in, up_in, down_in,
    mixed, token_grad, gate_grad, out_g, out_u, out_d,
    all_g, all_u, all_d, down_full,
    send_rows, recv_rows, send_back, recv_back,
    hidden, pre_grads,
    part_g, part_u, part_d, sum_g, sum_u, sum_d,
    ag_send, ag_recv, pass_send, pass_recv,
    rs_send, rs_recv, push_send, push_recv,
    a2a_send, a2a_recv, back_send, back_recv,
):
    rows_tok, width = tok.shape
    planes = 2 * NX * NY
    nz = 2 * NZL
    slots = planes * CAP
    ff = gate_in.shape[-1]

    dp, ex = lax.axis_index("dp"), lax.axis_index("expert")
    zl, c = lax.div(dp, 2), lax.rem(dp, 2)
    y, zh, x = lax.div(ex, 2 * NX), lax.rem(lax.div(ex, NX), 2), lax.rem(ex, NX)
    z = zh * NZL + zl
    half = NX * NY
    spot = y * NX + x
    me = c * half + spot

    def along_z(zz, core):
        return (lax.rem(zz, NZL) * 2 + core, y * (2 * NX) + lax.div(zz, NZL) * NX + x)

    def in_plane(q):
        qc, qy, qx = lax.div(q, half), lax.rem(lax.div(q, NX), NY), lax.rem(q, NX)
        return (zl * 2 + qc, qy * (2 * NX) + zh * NX + qx)

    ring = (along_z(lax.rem(z + 1, nz), c), along_z(lax.rem(z + nz - 1, nz), c))
    other = along_z(z, 1 - c)

    def far(flow, core):
        return NZL - lax.rem(core + flow, 2)

    def source(flow, hops):
        return lax.rem(z - hops + nz, nz) if flow == 0 else lax.rem(z + hops, nz)

    def target(flow, hops):
        return source(1 - flow, hops)

    def family(zz):
        return lax.div(zz, NZL)

    def mixed_order(o):
        dx = lax.rem(o, NX)
        dy = lax.rem(lax.div(o, NX) + dx, NY)
        return lax.rem(y + dy, NY) * NX + lax.rem(x + dx, NX)

    def remote(src, dst, send_sem, recv_sem, device):
        return pltpu.make_async_remote_copy(
            src_ref=src, dst_ref=dst, send_sem=send_sem, recv_sem=recv_sem,
            device_id=device, device_id_type=pl.DeviceIdType.MESH,
        )

    barrier = pltpu.get_barrier_semaphore()

    def greet(o, _):
        pl.semaphore_signal(
            barrier, inc=1, device_id=in_plane(lax.rem(me + o, planes)),
            device_id_type=pl.DeviceIdType.MESH,
        )
        return 0

    for device in ring:
        pl.semaphore_signal(
            barrier, inc=1, device_id=device, device_id_type=pl.DeviceIdType.MESH
        )
    lax.fori_loop(1, planes, greet, 0)
    pl.semaphore_wait(barrier, planes + 1)

    shards_in, gathered = (gate_in, up_in, down_in), (all_g, all_u, all_d)
    first_own = c * nz

    def ag_copy(q, flow, zz):
        at = gathered[q].at[2 * zz + c]
        return remote(at, at, ag_send.at[flow, zz, q], ag_recv.at[zz, q], ring[flow])

    def pass_copy(q, zz):
        at = gathered[q].at[2 * zz + c]
        return remote(
            at, at, pass_send.at[lax.rem(zz, NZL), q], pass_recv.at[lax.rem(zz, NZL), q], other
        )

    def pass_on(q, zz):
        @pl.when(family(zz) != c)
        def _():
            pass_copy(q, zz).start()

    for q in range(3):
        gathered[q][2 * z + c] = shards_in[q][0]
        for flow in (0, 1):
            ag_copy(q, flow, z).start()
        pass_on(q, z)

    def forward(s):
        for q in range(3):
            for flow in (0, 1):
                zz = source(flow, s)

                def arrived(q=q, flow=flow, zz=zz):
                    ag_copy(q, flow, zz).wait_recv()

                def onward(q=q, flow=flow, zz=zz):
                    ag_copy(q, flow, zz).start()

                if s < NZL - 1:
                    arrived()
                    onward()
                    pass_on(q, zz)
                elif s == NZL - 1:
                    arrived()
                    pl.when(far(flow, c) == NZL)(onward)
                    pass_on(q, zz)
                else:

                    @pl.when(far(flow, c) == NZL)
                    def _(q=q, zz=zz, arrived=arrived):
                        arrived()
                        pass_on(q, zz)

    eye = lax.broadcasted_iota(jnp.int32, (rows_tok, rows_tok), 0) == lax.broadcasted_iota(
        jnp.int32, (rows_tok, rows_tok), 1
    )

    def column(row):
        return jnp.sum(jnp.where(eye, row, 0.0), axis=1, keepdims=True)

    def row_of(col):
        return jnp.sum(jnp.where(eye, col, 0.0), axis=0, keepdims=True)

    alive = lax.broadcasted_iota(jnp.int32, (rows_tok, 1), 0) < live[0]
    lanes = lax.broadcasted_iota(jnp.int32, (rows_tok, planes), 1).astype(F32)
    earlier = (
        lax.broadcasted_iota(jnp.int32, (rows_tok, rows_tok), 1)
        < lax.broadcasted_iota(jnp.int32, (rows_tok, rows_tok), 0)
    ).astype(BF)
    slot, weight = [], []
    taken = jnp.zeros((1, planes), F32)
    for k in range(2):
        named = routing[k : k + 1, :]
        qy, qc, qx = lax.div(named, 2 * NX), lax.rem(lax.div(named, NX), 2), lax.rem(named, NX)
        expert = column((qc * half + qy * NX + qx).astype(F32))
        weight.append(column(gates[k : k + 1, :]))
        onehot = jnp.where((expert == lanes) & alive, 1.0, 0.0)
        before = dot(earlier, onehot.astype(BF)) + taken
        taken = taken + jnp.sum(onehot, axis=0, keepdims=True)
        found = jnp.sum(onehot * (before + lanes * CAP), axis=1, keepdims=True)
        slot.append(jnp.where(alive, found, -1.0).astype(jnp.int32))

    def picks(k, start, count):
        at = lax.broadcasted_iota(jnp.int32, (rows_tok, count), 1) + start
        return jnp.where(slot[k] == at, 1.0, 0.0).astype(BF)

    scaled = [(weight[k] * cot[...].astype(F32)).astype(BF) for k in range(2)]

    def dispatch(q):
        return remote(send_rows.at[q], recv_rows.at[me], a2a_send, a2a_recv, in_plane(q))

    for j in range(2):
        first = lax.rem(c + j, 2) * half
        p0, p1 = (picks(k, first * CAP, half * CAP) for k in range(2))
        shape = (half, CAP, width)
        send_rows[pl.ds(first, half), 0] = contract_first(p0 + p1, tok[...]).astype(BF).reshape(shape)
        send_rows[pl.ds(first, half), 1] = (
            (contract_first(p0, scaled[0]) + contract_first(p1, scaled[1])).astype(BF).reshape(shape)
        )

        def send(o, _, first=first):
            q = first + mixed_order(o)

            @pl.when(q != me)
            def _():
                dispatch(q).start()

            return 0

        lax.fori_loop(0, half, send, 0)
        if j + 1 <= NZL:
            forward(j + 1)
    recv_rows[me] = send_rows[me]

    for s in range(3, NZL + 1):
        forward(s)

    def passed(b, _):
        for q in range(3):
            at = gathered[q].at[first_own + 2 * b + 1 - c]
            pltpu.make_async_copy(at, at, pass_recv.at[b, q]).wait()
        return 0

    lax.fori_loop(0, NZL, passed, 0)

    shard_rows = down_in.shape[1]
    for i in range(nz):
        down_full[i * shard_rows : (i + 1) * shard_rows] = all_d[first_own + i]

    def all_of(ref, sem, count):
        part = ref.at[pl.ds(0, count)]
        pltpu.make_async_copy(part, part, sem).wait()

    all_of(recv_rows, a2a_recv, planes - 1)

    tiles = 2
    per = planes // tiles
    tile_rows = per * CAP

    def gate_up():
        mine = pl.ds(first_own, nz)
        return all_g[mine].reshape(width, ff), all_u[mine].reshape(width, ff)

    def inner(t, _):
        first = t * per
        rows = pl.ds(pl.multiple_of(first * CAP, tile_rows), tile_rows)
        xs = recv_rows[pl.ds(first, per), 0].reshape(tile_rows, width)
        cs = recv_rows[pl.ds(first, per), 1].reshape(tile_rows, width)
        gate_w, up_w = gate_up()
        pre_gate = dot(xs, gate_w)
        pre_up = dot(xs, up_w)
        hidden_grad = contract_last(cs, down_full[...])
        sig = jax.nn.sigmoid(pre_gate)
        swish = pre_gate * sig
        hidden[rows] = (swish * pre_up).astype(BF)
        pre_grads[rows, :ff] = (
            hidden_grad * pre_up * sig * (1.0 + pre_gate * (1.0 - sig))
        ).astype(BF)
        pre_grads[rows, ff:] = (hidden_grad * swish).astype(BF)
        return 0

    lax.fori_loop(0, tiles, inner, 0)

    parts, sums = (part_g, part_u, part_d), (sum_g, sum_u, sum_d)
    mine = pl.ds(first_own, nz)
    both = contract_first(recv_rows[:, 0].reshape(slots, width), pre_grads[...])
    shape = (nz, width // nz, ff)
    part_g[mine] = both[:, :ff].astype(BF).reshape(shape)
    part_u[mine] = both[:, ff:].astype(BF).reshape(shape)
    down_grad = contract_first(hidden[...], recv_rows[:, 1].reshape(slots, width))
    for i in range(nz):
        part_d[first_own + i] = down_grad[i * shard_rows : (i + 1) * shard_rows].astype(BF)

    def push_copy(q, zz):
        at, b = parts[q].at[2 * zz + 1 - c], lax.rem(zz, NZL)
        return remote(at, at, push_send.at[b, q], push_recv.at[b, q], other)

    def pushed(q, zz):
        @pl.when(family(zz) != c)
        def _():
            at = parts[q].at[2 * zz + c]
            pltpu.make_async_copy(at, at, push_recv.at[lax.rem(zz, NZL), q]).wait()

    def push(s, _):
        for q in range(3):
            for flow in (0, 1):
                left = far(flow, 1 - c) - s
                zz = target(flow, left)

                @pl.when((family(zz) == c) & (left > 0))
                def _(q=q, zz=zz):
                    push_copy(q, zz).start()

        return 0

    lax.fori_loop(0, NZL, push, 0)
    for q in range(3):

        @pl.when(zh == c)
        def _(q=q):
            push_copy(q, z).start()

    def rs_copy(q, flow, zz, src):
        return remote(
            src, sums[q].at[flow, zz], rs_send.at[flow, zz, q], rs_recv.at[flow, zz, q], ring[flow]
        )

    def summing(left):
        for q in range(3):
            for flow in (0, 1):
                zz = target(flow, left)

                def begin(q=q, flow=flow, zz=zz):
                    pushed(q, zz)
                    rs_copy(q, flow, zz, parts[q].at[2 * zz + c]).start()

                def add(q=q, flow=flow, zz=zz):
                    at = sums[q].at[flow, zz]
                    pushed(q, zz)
                    rs_copy(q, flow, zz, at).wait_recv()
                    sums[q][flow, zz] = (
                        sums[q][flow, zz].astype(F32) + parts[q][2 * zz + c].astype(F32)
                    ).astype(BF)
                    rs_copy(q, flow, zz, at).start()

                farthest = far(flow, c) == NZL
                if left == NZL:
                    pl.when(farthest)(begin)
                elif left == NZL - 1:
                    pl.when(jnp.logical_not(farthest))(begin)
                    pl.when(farthest)(add)
                else:
                    add()

    summing(NZL)

    def combine(q):
        return remote(send_back.at[q], recv_back.at[me], back_send, back_recv, in_plane(q))

    def outer(t, _):
        first = lax.rem(t + c, tiles) * per
        rows = pl.ds(pl.multiple_of(first * CAP, tile_rows), tile_rows)
        gate_w, up_w = gate_up()
        shape = (per, CAP, width)
        send_back[pl.ds(first, per), 0] = dot(hidden[rows], down_full[...]).astype(BF).reshape(shape)
        part = contract_last(pre_grads[rows, :ff], gate_w)
        part += contract_last(pre_grads[rows, ff:], up_w)
        send_back[pl.ds(first, per), 1] = part.astype(BF).reshape(shape)

        def send(o, _):
            q = first + mixed_order(o)

            @pl.when(q != me)
            def _():
                combine(q).start()

            return 0

        lax.fori_loop(0, per, send, 0)
        return 0

    lax.fori_loop(0, tiles, outer, 0)
    recv_back[me] = send_back[me]
    for left in range(NZL - 1, 0, -1):
        summing(left)

    all_of(recv_back, back_recv, planes - 1)
    p0, p1 = (picks(k, 0, slots) for k in range(2))
    token_grad[...] = dot(p0 + p1, recv_back[:, 1].reshape(slots, width)).astype(BF)
    total = jnp.zeros((rows_tok, width), F32)
    cot_f = cot[...].astype(F32)
    for k, p in enumerate((p0, p1)):
        got = dot(p, recv_back[:, 0].reshape(slots, width))
        total += weight[k] * got
        gate_grad[k : k + 1, :] = row_of(jnp.sum(cot_f * got, axis=1, keepdims=True))
    mixed[...] = total.astype(BF)

    outs = (out_g, out_u, out_d)
    for q in range(3):
        pushed(q, z)
        total = parts[q][2 * z + c].astype(F32)
        for flow in (0, 1):
            rs_copy(q, flow, z, sums[q].at[flow, z]).wait_recv()
            total += sums[q][flow, z].astype(F32)
        outs[q][0] = (total * (1.0 / nz)).astype(BF)

    def sent(s, _):
        for q in range(3):
            for flow in (0, 1):

                @pl.when(s < far(flow, c))
                def _(q=q, flow=flow):
                    ag_copy(q, flow, source(flow, s)).wait_send()
                    zz = target(flow, s + 1)
                    rs_copy(q, flow, zz, parts[q].at[2 * zz + c]).wait_send()

            pass_copy(q, (1 - c) * NZL + s).wait_send()
            push_copy(q, c * NZL + s).wait_send()
        return 0

    lax.fori_loop(0, NZL, sent, 0)
    all_of(send_rows, a2a_send, planes - 1)
    all_of(send_back, back_send, planes - 1)


def hand_over(*refs):
    half = len(refs) // 2
    for i in range(half):
        refs[half + i][...] = refs[i][...]


def shards(
    tokens, cotangent, routing, gate_values, live_counts, gate_weights, up_weights, down_weights
):
    rows_tok, width = tokens.shape
    ff = gate_weights.shape[-1]
    planes, nz = 2 * NX * NY, 2 * NZL
    slots = planes * CAP
    shapes = [gate_weights.shape[1:], up_weights.shape[1:], down_weights.shape[1:]]
    vmem = pl.BlockSpec(memory_space=pltpu.VMEM)
    dma = pltpu.SemaphoreType.DMA
    block = pltpu.VMEM((planes, 2, CAP, width), BF)
    flops = 18 * slots * width * ff
    outs = pl.pallas_call(
        kernel,
        out_shape=(
            jax.ShapeDtypeStruct((rows_tok, width), BF),
            jax.ShapeDtypeStruct((rows_tok, width), BF),
            jax.ShapeDtypeStruct((2, rows_tok), F32),
            *(jax.ShapeDtypeStruct((1, *s), BF) for s in shapes),
        ),
        in_specs=[vmem] * 4 + [pl.BlockSpec(memory_space=pltpu.SMEM)] + [vmem] * 3,
        out_specs=tuple([vmem] * 6),
        scratch_shapes=[
            *(pltpu.VMEM((2 * nz, *s), BF) for s in shapes),
            pltpu.VMEM((ff, width), BF),
            *([block] * 4),
            pltpu.VMEM((slots, ff), BF),
            pltpu.VMEM((slots, 2 * ff), BF),
            *(pltpu.VMEM((2 * nz, *s), BF) for s in shapes),
            *(pltpu.VMEM((2, nz, *s), BF) for s in shapes),
            dma((2, nz, 3)),
            dma((nz, 3)),
            dma((NZL, 3)),
            dma((NZL, 3)),
            dma((2, nz, 3)),
            dma((2, nz, 3)),
            dma((NZL, 3)),
            dma((NZL, 3)),
            dma,
            dma,
            dma,
            dma,
        ],
        compiler_params=pltpu.CompilerParams(
            collective_id=0, has_side_effects=True, vmem_limit_bytes=56 * 1024 * 1024
        ),
        cost_estimate=pl.CostEstimate(
            flops=flops, bytes_accessed=2 * 1024 * 1024, transcendentals=slots * ff
        ),
    )(
        tokens, cotangent, routing.T, gate_values.T, live_counts,
        gate_weights, up_weights, down_weights,
    )
    outs = pl.pallas_call(
        hand_over,
        out_shape=tuple(jax.ShapeDtypeStruct(o.shape, o.dtype) for o in outs),
        in_specs=[vmem] * len(outs),
        out_specs=tuple([vmem] * len(outs)),
    )(*outs)
    mixed, token_grad, gate_grad, grad_g, grad_u, grad_d = outs
    return mixed, token_grad, gate_grad.T, grad_g, grad_u, grad_d


def solution(mesh):
    return jax.shard_map(
        shards,
        mesh=mesh,
        in_specs=(
            P(("dp", "expert"), None),
            P(("dp", "expert"), None),
            P(("dp", "expert"), None),
            P(("dp", "expert"), None),
            P(("dp", "expert")),
            P("expert", "dp", None),
            P("expert", "dp", None),
            P("expert", "dp", None),
        ),
        out_specs=(
            P(("dp", "expert"), None),
            P(("dp", "expert"), None),
            P(("dp", "expert"), None),
            P("expert", "dp", None),
            P("expert", "dp", None),
            P("expert", "dp", None),
        ),
        check_vma=False,
    )
```

```python
import functools

import jax
import jax.numpy as jnp
from jax import lax
from jax.experimental import pallas as pl
from jax.experimental.pallas import tpu as pltpu
from jax.sharding import PartitionSpec as P

NX, NY, NZL = 4, 4, 8
CAP = 16
BF, F32 = jnp.bfloat16, jnp.float32


def contract_last(left, right):
    return lax.dot_general(
        left, right, (((1,), (1,)), ((), ())), preferred_element_type=F32
    )


def contract_first(left, right):
    return lax.dot_general(
        left, right, (((0,), (0,)), ((), ())), preferred_element_type=F32
    )


def dot(left, right):
    return jnp.dot(left, right, preferred_element_type=F32)


def kernel(
    tok_in, cot_in, routing, gates, live,
    gate_in, up_in, down_in,
    mixed, token_grad, gate_grad, out_g, out_u, out_d,
    tok, cot, all_g, all_u, all_d, down_full,
    send_rows, recv_rows, send_back, recv_back,
    hidden, pre_grads,
    part_g, part_u, part_d, sum_g, sum_u, sum_d,
    load_rows, load_shards, ag_send, arrival, pass_send,
    rs_send, rs_recv, rs_first, push_send, push_recv,
    a2a_send, a2a_recv, back_send, back_recv,
):
    rows_tok, width = tok.shape
    planes = 2 * NX * NY
    nz = 2 * NZL
    slots = planes * CAP
    ff = gate_in.shape[-1]

    dp, ex = lax.axis_index("dp"), lax.axis_index("expert")
    zl, c = lax.div(dp, 2), lax.rem(dp, 2)
    y, zh, x = lax.div(ex, 2 * NX), lax.rem(lax.div(ex, NX), 2), lax.rem(ex, NX)
    z = zh * NZL + zl
    half = NX * NY
    spot = y * NX + x
    me = c * half + spot

    def along_z(zz, core):
        return (lax.rem(zz, NZL) * 2 + core, y * (2 * NX) + lax.div(zz, NZL) * NX + x)

    def in_plane(q):
        qc, qy, qx = lax.div(q, half), lax.rem(lax.div(q, NX), NY), lax.rem(q, NX)
        return (zl * 2 + qc, qy * (2 * NX) + zh * NX + qx)

    beside = (lax.rem(z + 1, nz), lax.rem(z + nz - 1, nz))
    ring = tuple(along_z(zz, c) for zz in beside)
    other = along_z(z, 1 - c)

    def far(flow, core):
        return NZL - lax.rem(core + flow, 2)

    def source(flow, hops):
        return lax.rem(z - hops + nz, nz) if flow == 0 else lax.rem(z + hops, nz)

    def target(flow, hops):
        return source(1 - flow, hops)

    def family(zz):
        return lax.div(zz, NZL)

    def mixed_order(o):
        dx = lax.rem(o, NX)
        dy = lax.rem(lax.div(o, NX) + dx, NY)
        return lax.rem(y + dy, NY) * NX + lax.rem(x + dx, NX)

    def remote(src, dst, send_sem, recv_sem, device):
        return pltpu.make_async_remote_copy(
            src_ref=src, dst_ref=dst, send_sem=send_sem, recv_sem=recv_sem,
            device_id=device, device_id_type=pl.DeviceIdType.MESH,
        )

    shards_in, gathered = (gate_in, up_in, down_in), (all_g, all_u, all_d)
    load = [
        pltpu.make_async_copy(shards_in[q].at[0], gathered[q].at[2 * z + c], load_shards.at[q])
        for q in range(3)
    ]
    load += [
        pltpu.make_async_copy(tok_in, tok, load_rows.at[0]),
        pltpu.make_async_copy(cot_in, cot, load_rows.at[1]),
    ]
    for copy in load:
        copy.start()

    barrier = pltpu.get_barrier_semaphore()

    def greet(o, _):
        pl.semaphore_signal(
            barrier, inc=1, device_id=in_plane(lax.rem(me + o, planes)),
            device_id_type=pl.DeviceIdType.MESH,
        )
        return 0

    for device in (*ring, *(along_z(zz, 1 - c) for zz in beside)):
        pl.semaphore_signal(
            barrier, inc=1, device_id=device, device_id_type=pl.DeviceIdType.MESH
        )
    lax.fori_loop(1, planes, greet, 0)
    pl.semaphore_wait(barrier, planes + 3)

    first_own = c * nz

    def ag_copy(q, flow, zz, core):
        at = gathered[q].at[2 * zz + c]
        return remote(
            at, at, ag_send.at[flow, zz, q], arrival.at[2 * zz + c, q], along_z(beside[flow], core)
        )

    def pass_copy(q, zz):
        at = gathered[q].at[2 * zz + c]
        return remote(
            at, at, pass_send.at[lax.rem(zz, NZL), q], arrival.at[2 * zz + c, q], other
        )

    def onward(q, flow, s, zz):
        if s + 1 < NZL - 1:
            ag_copy(q, flow, zz, c).start()
        elif s + 1 == NZL - 1:
            last = far(flow, c) == NZL - 1
            ag_copy(q, flow, zz, jnp.where(last, family(zz), c)).start()
        else:

            @pl.when(far(flow, c) == NZL)
            def _():
                ag_copy(q, flow, zz, family(zz)).start()

    def forward(s):
        for q in range(3):
            for flow in (0, 1):
                zz = source(flow, s)

                def arrived(q=q, flow=flow, zz=zz):
                    ag_copy(q, flow, zz, c).wait_recv()

                def pass_on(q=q, zz=zz):
                    @pl.when(family(zz) != c)
                    def _():
                        pass_copy(q, zz).start()

                if s < NZL - 1:
                    arrived()
                    onward(q, flow, s, zz)
                    pass_on()
                elif s == NZL - 1:
                    ends = far(flow, c) == s

                    @pl.when(jnp.logical_not(ends))
                    def _(q=q, flow=flow, zz=zz, arrived=arrived, pass_on=pass_on):
                        arrived()
                        onward(q, flow, s, zz)
                        pass_on()

                    pl.when(ends & (family(zz) == c))(arrived)
                else:
                    pl.when((far(flow, c) == s) & (family(zz) == c))(arrived)

    for q in range(3):
        load[q].wait()
        for flow in (0, 1):
            onward(q, flow, 0, z)

        @pl.when(zh != c)
        def _(q=q):
            pass_copy(q, z).start()

    eye = lax.broadcasted_iota(jnp.int32, (rows_tok, rows_tok), 0) == lax.broadcasted_iota(
        jnp.int32, (rows_tok, rows_tok), 1
    )

    def column(row):
        return jnp.sum(jnp.where(eye, row, 0.0), axis=1, keepdims=True)

    def row_of(col):
        return jnp.sum(jnp.where(eye, col, 0.0), axis=0, keepdims=True)

    alive = lax.broadcasted_iota(jnp.int32, (rows_tok, 1), 0) < live[0]
    lanes = lax.broadcasted_iota(jnp.int32, (rows_tok, planes), 1).astype(F32)
    earlier = (
        lax.broadcasted_iota(jnp.int32, (rows_tok, rows_tok), 1)
        < lax.broadcasted_iota(jnp.int32, (rows_tok, rows_tok), 0)
    ).astype(BF)
    slot, weight = [], []
    taken = jnp.zeros((1, planes), F32)
    for k in range(2):
        named = routing[k : k + 1, :]
        qy, qc, qx = lax.div(named, 2 * NX), lax.rem(lax.div(named, NX), 2), lax.rem(named, NX)
        expert = column((qc * half + qy * NX + qx).astype(F32))
        weight.append(column(gates[k : k + 1, :]))
        onehot = jnp.where((expert == lanes) & alive, 1.0, 0.0)
        before = dot(earlier, onehot.astype(BF)) + taken
        taken = taken + jnp.sum(onehot, axis=0, keepdims=True)
        found = jnp.sum(onehot * (before + lanes * CAP), axis=1, keepdims=True)
        slot.append(jnp.where(alive, found, -1.0).astype(jnp.int32))

    def picks(k, start, count):
        at = lax.broadcasted_iota(jnp.int32, (rows_tok, count), 1) + start
        return jnp.where(slot[k] == at, 1.0, 0.0).astype(BF)

    load[3].wait()
    load[4].wait()
    scaled = [(weight[k] * cot[...].astype(F32)).astype(BF) for k in range(2)]

    def dispatch(q):
        return remote(send_rows.at[q], recv_rows.at[me], a2a_send, a2a_recv, in_plane(q))

    for j in range(2):
        first = lax.rem(c + j, 2) * half
        p0, p1 = (picks(k, first * CAP, half * CAP) for k in range(2))
        shape = (half, CAP, width)
        send_rows[pl.ds(first, half), 0] = contract_first(p0 + p1, tok[...]).astype(BF).reshape(shape)
        send_rows[pl.ds(first, half), 1] = (
            (contract_first(p0, scaled[0]) + contract_first(p1, scaled[1])).astype(BF).reshape(shape)
        )

        def send(o, _, first=first):
            q = first + mixed_order(o)

            @pl.when(q != me)
            def _():
                dispatch(q).start()

            return 0

        lax.fori_loop(0, half, send, 0)
        if j + 1 <= NZL:
            forward(j + 1)
    recv_rows[me] = send_rows[me]

    for s in range(3, NZL + 1):
        forward(s)

    def passed(b, _):
        for q in range(3):
            place = first_own + 2 * b + 1 - c
            at = gathered[q].at[place]
            pltpu.make_async_copy(at, at, arrival.at[place, q]).wait()
        return 0

    lax.fori_loop(0, NZL, passed, 0)

    shard_rows = down_in.shape[1]
    for i in range(nz):
        down_full[i * shard_rows : (i + 1) * shard_rows] = all_d[first_own + i]

    def all_of(ref, sem, count):
        part = ref.at[pl.ds(0, count)]
        pltpu.make_async_copy(part, part, sem).wait()

    all_of(recv_rows, a2a_recv, planes - 1)

    tiles = 2
    per = planes // tiles
    tile_rows = per * CAP

    def gate_up():
        mine = pl.ds(first_own, nz)
        return all_g[mine].reshape(width, ff), all_u[mine].reshape(width, ff)

    def inner(t, _):
        first = t * per
        rows = pl.ds(pl.multiple_of(first * CAP, tile_rows), tile_rows)
        xs = recv_rows[pl.ds(first, per), 0].reshape(tile_rows, width)
        cs = recv_rows[pl.ds(first, per), 1].reshape(tile_rows, width)
        gate_w, up_w = gate_up()
        pre_gate = dot(xs, gate_w)
        pre_up = dot(xs, up_w)
        hidden_grad = contract_last(cs, down_full[...])
        sig = jax.nn.sigmoid(pre_gate)
        swish = pre_gate * sig
        hidden[rows] = (swish * pre_up).astype(BF)
        pre_grads[rows, :ff] = (
            hidden_grad * pre_up * sig * (1.0 + pre_gate * (1.0 - sig))
        ).astype(BF)
        pre_grads[rows, ff:] = (hidden_grad * swish).astype(BF)
        return 0

    lax.fori_loop(0, tiles, inner, 0)

    parts, sums = (part_g, part_u, part_d), (sum_g, sum_u, sum_d)
    mine = pl.ds(first_own, nz)
    both = contract_first(recv_rows[:, 0].reshape(slots, width), pre_grads[...])
    shape = (nz, width // nz, ff)
    part_g[mine] = both[:, :ff].astype(BF).reshape(shape)
    part_u[mine] = both[:, ff:].astype(BF).reshape(shape)
    down_grad = contract_first(hidden[...], recv_rows[:, 1].reshape(slots, width))
    for i in range(nz):
        part_d[first_own + i] = down_grad[i * shard_rows : (i + 1) * shard_rows].astype(BF)

    def push_copy(q, zz):
        at, b = parts[q].at[2 * zz + 1 - c], lax.rem(zz, NZL)
        return remote(at, at, push_send.at[b, q], push_recv.at[b, q], other)

    def pushed(q, zz):
        @pl.when(family(zz) != c)
        def _():
            at = parts[q].at[2 * zz + c]
            pltpu.make_async_copy(at, at, push_recv.at[lax.rem(zz, NZL), q]).wait()

    def first_copy(q, flow, h, core):
        zz = target(flow, far(flow, core))
        return family(zz) == c, remote(
            parts[q].at[2 * zz + core], sums[q].at[flow, zz], rs_first.at[flow, h, q],
            rs_recv.at[flow, zz, q], along_z(beside[flow], core),
        )

    for q in range(3):
        for flow in (0, 1):
            for h, core in enumerate((c, 1 - c)):
                ours, copy = first_copy(q, flow, h, core)
                pl.when(ours)(copy.start)

    def each_push(do):
        def some(s, _):
            for q in range(3):
                for flow in (0, 1):
                    left = far(flow, 1 - c) - s
                    zz = target(flow, left)

                    @pl.when((family(zz) == c) & (left > 0))
                    def _(q=q, zz=zz):
                        do(push_copy(q, zz))

            return 0

        lax.fori_loop(1, NZL, some, 0)

        @pl.when(zh == c)
        def _():
            for q in range(3):
                do(push_copy(q, z))

    each_push(lambda copy: copy.start())

    def rs_copy(q, flow, zz, src):
        return remote(
            src, sums[q].at[flow, zz], rs_send.at[flow, zz, q], rs_recv.at[flow, zz, q], ring[flow]
        )

    def summing(left):
        for q in range(3):
            for flow in (0, 1):
                zz = target(flow, left)

                def add(q=q, flow=flow, zz=zz):
                    at = sums[q].at[flow, zz]
                    pushed(q, zz)
                    rs_copy(q, flow, zz, at).wait_recv()
                    sums[q][flow, zz] = (
                        sums[q][flow, zz].astype(F32) + parts[q][2 * zz + c].astype(F32)
                    ).astype(BF)
                    rs_copy(q, flow, zz, at).start()

                farthest = far(flow, c) == NZL
                if left == NZL - 1:
                    pl.when(farthest)(add)
                else:
                    add()

    def combine(q):
        return remote(send_back.at[q], recv_back.at[me], back_send, back_recv, in_plane(q))

    def outer(t, _):
        first = lax.rem(t + c, tiles) * per
        rows = pl.ds(pl.multiple_of(first * CAP, tile_rows), tile_rows)
        gate_w, up_w = gate_up()
        shape = (per, CAP, width)
        send_back[pl.ds(first, per), 0] = dot(hidden[rows], down_full[...]).astype(BF).reshape(shape)
        part = contract_last(pre_grads[rows, :ff], gate_w)
        part += contract_last(pre_grads[rows, ff:], up_w)
        send_back[pl.ds(first, per), 1] = part.astype(BF).reshape(shape)

        def send(o, _):
            q = first + mixed_order(o)

            @pl.when(q != me)
            def _():
                combine(q).start()

            return 0

        lax.fori_loop(0, per, send, 0)
        return 0

    lax.fori_loop(0, tiles, outer, 0)
    recv_back[me] = send_back[me]
    for left in range(NZL - 1, 0, -1):
        summing(left)

    all_of(recv_back, back_recv, planes - 1)
    p0, p1 = (picks(k, 0, slots) for k in range(2))
    token_grad[...] = dot(p0 + p1, recv_back[:, 1].reshape(slots, width)).astype(BF)
    total = jnp.zeros((rows_tok, width), F32)
    cot_f = cot[...].astype(F32)
    for k, p in enumerate((p0, p1)):
        got = dot(p, recv_back[:, 0].reshape(slots, width))
        total += weight[k] * got
        gate_grad[k : k + 1, :] = row_of(jnp.sum(cot_f * got, axis=1, keepdims=True))
    mixed[...] = total.astype(BF)

    outs = (out_g, out_u, out_d)
    for q in range(3):
        pushed(q, z)
        total = parts[q][2 * z + c].astype(F32)
        for flow in (0, 1):
            rs_copy(q, flow, z, sums[q].at[flow, z]).wait_recv()
            total += sums[q][flow, z].astype(F32)
        outs[q][0] = (total * (1.0 / nz)).astype(BF)

    def sent(s, _):
        for q in range(3):
            for flow in (0, 1):
                zz = source(flow, s)

                @pl.when(s < far(flow, c))
                def _(q=q, flow=flow, zz=zz):
                    ag_copy(q, flow, zz, c).wait_send()

                    @pl.when((family(zz) != c) & ((s > 0) | (flow == 0)))
                    def _():
                        pass_copy(q, zz).wait_send()

                zz = target(flow, s + 1)

                @pl.when(s + 1 < far(flow, c))
                def _(q=q, flow=flow, zz=zz):
                    rs_copy(q, flow, zz, sums[q].at[flow, zz]).wait_send()

        return 0

    lax.fori_loop(0, NZL, sent, 0)
    each_push(lambda copy: copy.wait_send())
    for q in range(3):
        for flow in (0, 1):
            for h, core in enumerate((c, 1 - c)):
                ours, copy = first_copy(q, flow, h, core)
                pl.when(ours)(copy.wait_send)
    all_of(send_rows, a2a_send, planes - 1)
    all_of(send_back, back_send, planes - 1)


def hand_over(*refs):
    half = len(refs) // 2
    for i in range(half):
        refs[half + i][...] = refs[i][...]


def shards(
    tokens, cotangent, routing, gate_values, live_counts, gate_weights, up_weights, down_weights
):
    rows_tok, width = tokens.shape
    ff = gate_weights.shape[-1]
    planes, nz = 2 * NX * NY, 2 * NZL
    slots = planes * CAP
    shapes = [gate_weights.shape[1:], up_weights.shape[1:], down_weights.shape[1:]]
    vmem = pl.BlockSpec(memory_space=pltpu.VMEM)
    hbm = pl.BlockSpec(memory_space=pl.ANY)
    dma = pltpu.SemaphoreType.DMA
    block = pltpu.VMEM((planes, 2, CAP, width), BF)
    flops = 18 * slots * width * ff
    outs = pl.pallas_call(
        kernel,
        out_shape=(
            jax.ShapeDtypeStruct((rows_tok, width), BF),
            jax.ShapeDtypeStruct((rows_tok, width), BF),
            jax.ShapeDtypeStruct((2, rows_tok), F32),
            *(jax.ShapeDtypeStruct((1, *s), BF) for s in shapes),
        ),
        in_specs=[hbm] * 2 + [vmem] * 2 + [pl.BlockSpec(memory_space=pltpu.SMEM)] + [hbm] * 3,
        out_specs=tuple([vmem] * 6),
        scratch_shapes=[
            *([pltpu.VMEM((rows_tok, width), BF)] * 2),
            *(pltpu.VMEM((2 * nz, *s), BF) for s in shapes),
            pltpu.VMEM((ff, width), BF),
            *([block] * 4),
            pltpu.VMEM((slots, ff), BF),
            pltpu.VMEM((slots, 2 * ff), BF),
            *(pltpu.VMEM((2 * nz, *s), BF) for s in shapes),
            *(pltpu.VMEM((2, nz, *s), BF) for s in shapes),
            dma((2,)),
            dma((3,)),
            dma((2, nz, 3)),
            dma((2 * nz, 3)),
            dma((NZL, 3)),
            dma((2, nz, 3)),
            dma((2, nz, 3)),
            dma((2, 2, 3)),
            dma((NZL, 3)),
            dma((NZL, 3)),
            dma,
            dma,
            dma,
            dma,
        ],
        compiler_params=pltpu.CompilerParams(
            collective_id=0, has_side_effects=True, vmem_limit_bytes=56 * 1024 * 1024
        ),
        cost_estimate=pl.CostEstimate(
            flops=flops, bytes_accessed=2 * 1024 * 1024, transcendentals=slots * ff
        ),
    )(
        tokens, cotangent, routing.T, gate_values.T, live_counts,
        gate_weights, up_weights, down_weights,
    )
    outs = pl.pallas_call(
        hand_over,
        out_shape=tuple(jax.ShapeDtypeStruct(o.shape, o.dtype) for o in outs),
        in_specs=[vmem] * len(outs),
        out_specs=tuple([vmem] * len(outs)),
    )(*outs)
    mixed, token_grad, gate_grad, grad_g, grad_u, grad_d = outs
    return mixed, token_grad, gate_grad.T, grad_g, grad_u, grad_d


def solution(mesh):
    return jax.shard_map(
        shards,
        mesh=mesh,
        in_specs=(
            P(("dp", "expert"), None),
            P(("dp", "expert"), None),
            P(("dp", "expert"), None),
            P(("dp", "expert"), None),
            P(("dp", "expert")),
            P("expert", "dp", None),
            P("expert", "dp", None),
            P("expert", "dp", None),
        ),
        out_specs=(
            P(("dp", "expert"), None),
            P(("dp", "expert"), None),
            P(("dp", "expert"), None),
            P("expert", "dp", None),
            P("expert", "dp", None),
            P("expert", "dp", None),
        ),
        check_vma=False,
    )
```

```python
import functools

import jax
import jax.numpy as jnp
from jax import lax
from jax.experimental import pallas as pl
from jax.experimental.pallas import tpu as pltpu
from jax.sharding import PartitionSpec as P

NX, NY, NZL = 4, 4, 8
CAP = 16
BF, F32 = jnp.bfloat16, jnp.float32


def contract_last(left, right):
    return lax.dot_general(
        left, right, (((1,), (1,)), ((), ())), preferred_element_type=F32
    )


def contract_first(left, right):
    return lax.dot_general(
        left, right, (((0,), (0,)), ((), ())), preferred_element_type=F32
    )


def dot(left, right):
    return jnp.dot(left, right, preferred_element_type=F32)


def kernel(
    tok_in, cot_in, routing, gates, live,
    gate_in, up_in, down_in,
    mixed, token_grad, gate_grad, out_g, out_u, out_d,
    tok, cot, all_g, all_u, all_d, down_full,
    send_rows, recv_rows, send_back, recv_back,
    hidden, pre_grads,
    part_g, part_u, part_d, sum_g, sum_u, sum_d,
    load_rows, load_shards, ag_send, arrival, pass_send,
    rs_send, rs_recv, rs_first, push_send, push_recv,
    a2a_send, a2a_recv, back_send, back_recv,
):
    rows_tok, width = tok.shape
    planes = 2 * NX * NY
    nz = 2 * NZL
    slots = planes * CAP
    ff = gate_in.shape[-1]

    dp, ex = lax.axis_index("dp"), lax.axis_index("expert")
    zl, c = lax.div(dp, 2), lax.rem(dp, 2)
    y, zh, x = lax.div(ex, 2 * NX), lax.rem(lax.div(ex, NX), 2), lax.rem(ex, NX)
    z = zh * NZL + zl
    half = NX * NY
    spot = y * NX + x
    me = c * half + spot

    def along_z(zz, core):
        return (lax.rem(zz, NZL) * 2 + core, y * (2 * NX) + lax.div(zz, NZL) * NX + x)

    def in_plane(q):
        qc, qy, qx = lax.div(q, half), lax.rem(lax.div(q, NX), NY), lax.rem(q, NX)
        return (zl * 2 + qc, qy * (2 * NX) + zh * NX + qx)

    beside = (lax.rem(z + 1, nz), lax.rem(z + nz - 1, nz))
    ring = tuple(along_z(zz, c) for zz in beside)
    other = along_z(z, 1 - c)

    def far(flow, core):
        return NZL - lax.rem(core + flow, 2)

    def source(flow, hops):
        return lax.rem(z - hops + nz, nz) if flow == 0 else lax.rem(z + hops, nz)

    def target(flow, hops):
        return source(1 - flow, hops)

    def family(zz):
        return lax.div(zz, NZL)

    def mixed_order(o):
        dx = lax.rem(o, NX)
        dy = lax.rem(lax.div(o, NX) + dx, NY)
        return lax.rem(y + dy, NY) * NX + lax.rem(x + dx, NX)

    def remote(src, dst, send_sem, recv_sem, device):
        return pltpu.make_async_remote_copy(
            src_ref=src, dst_ref=dst, send_sem=send_sem, recv_sem=recv_sem,
            device_id=device, device_id_type=pl.DeviceIdType.MESH,
        )

    shards_in, gathered = (gate_in, up_in, down_in), (all_g, all_u, all_d)
    load = [
        pltpu.make_async_copy(shards_in[q].at[0], gathered[q].at[2 * z + c], load_shards.at[q])
        for q in range(3)
    ]
    load += [
        pltpu.make_async_copy(tok_in, tok, load_rows.at[0]),
        pltpu.make_async_copy(cot_in, cot, load_rows.at[1]),
    ]
    for copy in load:
        copy.start()

    barrier = pltpu.get_barrier_semaphore()

    def greet(o, _):
        pl.semaphore_signal(
            barrier, inc=1, device_id=in_plane(lax.rem(me + o, planes)),
            device_id_type=pl.DeviceIdType.MESH,
        )
        return 0

    for device in (*ring, *(along_z(zz, 1 - c) for zz in beside)):
        pl.semaphore_signal(
            barrier, inc=1, device_id=device, device_id_type=pl.DeviceIdType.MESH
        )
    lax.fori_loop(1, planes, greet, 0)
    pl.semaphore_wait(barrier, planes + 3)

    first_own = c * nz

    def ag_copy(q, flow, zz, core):
        at = gathered[q].at[2 * zz + c]
        place = jnp.where(core == c, zz, nz)
        return remote(at, at, ag_send.at[q], arrival.at[place, q], along_z(beside[flow], core))

    def pass_copy(q, zz):
        at = gathered[q].at[2 * zz + c]
        return remote(at, at, pass_send.at[q], arrival.at[nz, q], other)

    def onward(q, flow, s, zz):
        if s + 1 < NZL - 1:
            ag_copy(q, flow, zz, c).start()
        elif s + 1 == NZL - 1:
            last = far(flow, c) == NZL - 1
            ag_copy(q, flow, zz, jnp.where(last, family(zz), c)).start()
        else:

            @pl.when(far(flow, c) == NZL)
            def _():
                ag_copy(q, flow, zz, family(zz)).start()

    def forward(s):
        for q in range(3):
            for flow in (0, 1):
                zz = source(flow, s)

                def arrived(q=q, flow=flow, zz=zz):
                    ag_copy(q, flow, zz, c).wait_recv()

                def pass_on(q=q, zz=zz):
                    @pl.when(family(zz) != c)
                    def _():
                        pass_copy(q, zz).start()

                if s < NZL - 1:
                    arrived()
                    onward(q, flow, s, zz)
                    pass_on()
                elif s == NZL - 1:
                    ends = far(flow, c) == s

                    @pl.when(jnp.logical_not(ends))
                    def _(q=q, flow=flow, zz=zz, arrived=arrived, pass_on=pass_on):
                        arrived()
                        onward(q, flow, s, zz)
                        pass_on()

                    pl.when(ends & (family(zz) == c))(arrived)
                else:
                    pl.when((far(flow, c) == s) & (family(zz) == c))(arrived)

    for q in range(3):
        load[q].wait()
        for flow in (0, 1):
            onward(q, flow, 0, z)

        @pl.when(zh != c)
        def _(q=q):
            pass_copy(q, z).start()

    eye = lax.broadcasted_iota(jnp.int32, (rows_tok, rows_tok), 0) == lax.broadcasted_iota(
        jnp.int32, (rows_tok, rows_tok), 1
    )

    def column(row):
        return jnp.sum(jnp.where(eye, row, 0.0), axis=1, keepdims=True)

    def row_of(col):
        return jnp.sum(jnp.where(eye, col, 0.0), axis=0, keepdims=True)

    alive = lax.broadcasted_iota(jnp.int32, (rows_tok, 1), 0) < live[0]
    lanes = lax.broadcasted_iota(jnp.int32, (rows_tok, planes), 1).astype(F32)
    earlier = (
        lax.broadcasted_iota(jnp.int32, (rows_tok, rows_tok), 1)
        < lax.broadcasted_iota(jnp.int32, (rows_tok, rows_tok), 0)
    ).astype(BF)
    slot, weight = [], []
    taken = jnp.zeros((1, planes), F32)
    for k in range(2):
        named = routing[k : k + 1, :]
        qy, qc, qx = lax.div(named, 2 * NX), lax.rem(lax.div(named, NX), 2), lax.rem(named, NX)
        expert = column((qc * half + qy * NX + qx).astype(F32))
        weight.append(column(gates[k : k + 1, :]))
        onehot = jnp.where((expert == lanes) & alive, 1.0, 0.0)
        before = dot(earlier, onehot.astype(BF)) + taken
        taken = taken + jnp.sum(onehot, axis=0, keepdims=True)
        found = jnp.sum(onehot * (before + lanes * CAP), axis=1, keepdims=True)
        slot.append(jnp.where(alive, found, -1.0).astype(jnp.int32))

    def picks(k, start, count):
        at = lax.broadcasted_iota(jnp.int32, (rows_tok, count), 1) + start
        return jnp.where(slot[k] == at, 1.0, 0.0).astype(BF)

    load[3].wait()
    load[4].wait()
    scaled = [(weight[k] * cot[...].astype(F32)).astype(BF) for k in range(2)]

    def dispatch(q):
        return remote(send_rows.at[q], recv_rows.at[me], a2a_send, a2a_recv, in_plane(q))

    for j in range(2):
        first = lax.rem(c + j, 2) * half
        p0, p1 = (picks(k, first * CAP, half * CAP) for k in range(2))
        shape = (half, CAP, width)
        send_rows[pl.ds(first, half), 0] = contract_first(p0 + p1, tok[...]).astype(BF).reshape(shape)
        send_rows[pl.ds(first, half), 1] = (
            (contract_first(p0, scaled[0]) + contract_first(p1, scaled[1])).astype(BF).reshape(shape)
        )

        def send(o, _, first=first):
            q = first + mixed_order(o)

            @pl.when(q != me)
            def _():
                dispatch(q).start()

            return 0

        lax.fori_loop(0, half, send, 0)
        if j + 1 <= NZL:
            forward(j + 1)
    recv_rows[me] = send_rows[me]

    for s in range(3, NZL + 1):
        forward(s)

    def all_of(ref, sem, count):
        part = ref.at[pl.ds(0, count)]
        pltpu.make_async_copy(part, part, sem).wait()

    for q in range(3):
        all_of(gathered[q], arrival.at[nz, q], NZL)

    shard_rows = down_in.shape[1]
    for i in range(nz):
        down_full[i * shard_rows : (i + 1) * shard_rows] = all_d[first_own + i]

    all_of(recv_rows, a2a_recv, planes - 1)

    tiles = 2
    per = planes // tiles
    tile_rows = per * CAP

    def gate_up():
        mine = pl.ds(first_own, nz)
        return all_g[mine].reshape(width, ff), all_u[mine].reshape(width, ff)

    def inner(t, _):
        first = t * per
        rows = pl.ds(pl.multiple_of(first * CAP, tile_rows), tile_rows)
        xs = recv_rows[pl.ds(first, per), 0].reshape(tile_rows, width)
        cs = recv_rows[pl.ds(first, per), 1].reshape(tile_rows, width)
        gate_w, up_w = gate_up()
        pre_gate = dot(xs, gate_w)
        pre_up = dot(xs, up_w)
        hidden_grad = contract_last(cs, down_full[...])
        sig = jax.nn.sigmoid(pre_gate)
        swish = pre_gate * sig
        hidden[rows] = (swish * pre_up).astype(BF)
        pre_grads[rows, :ff] = (
            hidden_grad * pre_up * sig * (1.0 + pre_gate * (1.0 - sig))
        ).astype(BF)
        pre_grads[rows, ff:] = (hidden_grad * swish).astype(BF)
        return 0

    lax.fori_loop(0, tiles, inner, 0)

    parts, sums = (part_g, part_u, part_d), (sum_g, sum_u, sum_d)
    mine = pl.ds(first_own, nz)
    both = contract_first(recv_rows[:, 0].reshape(slots, width), pre_grads[...])
    shape = (nz, width // nz, ff)
    part_g[mine] = both[:, :ff].astype(BF).reshape(shape)
    part_u[mine] = both[:, ff:].astype(BF).reshape(shape)
    down_grad = contract_first(hidden[...], recv_rows[:, 1].reshape(slots, width))
    for i in range(nz):
        part_d[first_own + i] = down_grad[i * shard_rows : (i + 1) * shard_rows].astype(BF)

    def push_copy(q, zz):
        at, b = parts[q].at[2 * zz + 1 - c], lax.rem(zz, NZL)
        return remote(at, at, push_send.at[q], push_recv.at[b, q], other)

    def pushed(q, zz):
        @pl.when(family(zz) != c)
        def _():
            at = parts[q].at[2 * zz + c]
            pltpu.make_async_copy(at, at, push_recv.at[lax.rem(zz, NZL), q]).wait()

    def first_copy(q, flow, core):
        zz = target(flow, far(flow, core))
        return family(zz) == c, remote(
            parts[q].at[2 * zz + core], sums[q].at[flow, zz], rs_first.at[q],
            rs_recv.at[flow, zz, q], along_z(beside[flow], core),
        )

    for q in range(3):
        for flow in (0, 1):
            for core in (c, 1 - c):
                ours, copy = first_copy(q, flow, core)
                pl.when(ours)(copy.start)

    def push(s, _):
        for q in range(3):
            for flow in (0, 1):
                left = far(flow, 1 - c) - s
                zz = target(flow, left)

                @pl.when((family(zz) == c) & (left > 0))
                def _(q=q, zz=zz):
                    push_copy(q, zz).start()

        return 0

    lax.fori_loop(1, NZL, push, 0)

    @pl.when(zh == c)
    def _():
        for q in range(3):
            push_copy(q, z).start()

    def rs_copy(q, flow, zz, src):
        return remote(
            src, sums[q].at[flow, zz], rs_send.at[q], rs_recv.at[flow, zz, q], ring[flow]
        )

    def summing(left):
        for q in range(3):
            for flow in (0, 1):
                zz = target(flow, left)

                def add(q=q, flow=flow, zz=zz):
                    at = sums[q].at[flow, zz]
                    pushed(q, zz)
                    rs_copy(q, flow, zz, at).wait_recv()
                    sums[q][flow, zz] = (
                        sums[q][flow, zz].astype(F32) + parts[q][2 * zz + c].astype(F32)
                    ).astype(BF)
                    rs_copy(q, flow, zz, at).start()

                farthest = far(flow, c) == NZL
                if left == NZL - 1:
                    pl.when(farthest)(add)
                else:
                    add()

    def combine(q):
        return remote(send_back.at[q], recv_back.at[me], back_send, back_recv, in_plane(q))

    def outer(t, _):
        first = lax.rem(t + c, tiles) * per
        rows = pl.ds(pl.multiple_of(first * CAP, tile_rows), tile_rows)
        gate_w, up_w = gate_up()
        shape = (per, CAP, width)
        send_back[pl.ds(first, per), 0] = dot(hidden[rows], down_full[...]).astype(BF).reshape(shape)
        part = contract_last(pre_grads[rows, :ff], gate_w)
        part += contract_last(pre_grads[rows, ff:], up_w)
        send_back[pl.ds(first, per), 1] = part.astype(BF).reshape(shape)

        def send(o, _):
            q = first + mixed_order(o)

            @pl.when(q != me)
            def _():
                combine(q).start()

            return 0

        lax.fori_loop(0, per, send, 0)
        return 0

    left = NZL - 1
    for t in range(tiles):
        outer(t, 0)
        if left > 0:
            summing(left)
            left -= 1
    recv_back[me] = send_back[me]
    for hops in range(left, 0, -1):
        summing(hops)

    all_of(recv_back, back_recv, planes - 1)
    p0, p1 = (picks(k, 0, slots) for k in range(2))
    token_grad[...] = dot(p0 + p1, recv_back[:, 1].reshape(slots, width)).astype(BF)
    total = jnp.zeros((rows_tok, width), F32)
    cot_f = cot[...].astype(F32)
    for k, p in enumerate((p0, p1)):
        got = dot(p, recv_back[:, 0].reshape(slots, width))
        total += weight[k] * got
        gate_grad[k : k + 1, :] = row_of(jnp.sum(cot_f * got, axis=1, keepdims=True))
    mixed[...] = total.astype(BF)

    outs = (out_g, out_u, out_d)
    for q in range(3):
        pushed(q, z)
        total = parts[q][2 * z + c].astype(F32)
        for flow in (0, 1):
            rs_copy(q, flow, z, sums[q].at[flow, z]).wait_recv()
            total += sums[q][flow, z].astype(F32)
        outs[q][0] = (total * (1.0 / nz)).astype(BF)

    def count(flags):
        return sum(jnp.where(flag, 1, 0) for flag in flags)

    def drain(sem, number, least, most):
        for n in range(max(least, 1), most + 1):

            @pl.when(number == n)
            def _(n=n):
                for q in range(3):
                    all_of(gathered[q], sem.at[q], n)

    ends = [family(source(flow, far(flow, c))) != c for flow in (0, 1)]
    firsts = {core: [first_copy(0, flow, core)[0] for flow in (0, 1)] for core in (0, 1)}
    drain(pass_send, NZL - count(ends), NZL - 2, NZL)
    drain(
        push_send,
        NZL - count(family(target(flow, far(flow, 1 - c))) == c for flow in (0, 1)),
        NZL - 2,
        NZL,
    )
    drain(rs_first, count(firsts[0] + firsts[1]), 0, 4)
    for q in range(3):
        all_of(gathered[q], ag_send.at[q], 2 * NZL - 1)
        all_of(gathered[q], rs_send.at[q], 2 * NZL - 3)
    all_of(send_rows, a2a_send, planes - 1)
    all_of(send_back, back_send, planes - 1)


def hand_over(*refs):
    half = len(refs) // 2
    for i in range(half):
        refs[half + i][...] = refs[i][...]


def shards(
    tokens, cotangent, routing, gate_values, live_counts, gate_weights, up_weights, down_weights
):
    rows_tok, width = tokens.shape
    ff = gate_weights.shape[-1]
    planes, nz = 2 * NX * NY, 2 * NZL
    slots = planes * CAP
    shapes = [gate_weights.shape[1:], up_weights.shape[1:], down_weights.shape[1:]]
    vmem = pl.BlockSpec(memory_space=pltpu.VMEM)
    hbm = pl.BlockSpec(memory_space=pl.ANY)
    dma = pltpu.SemaphoreType.DMA
    block = pltpu.VMEM((planes, 2, CAP, width), BF)
    flops = 18 * slots * width * ff
    outs = pl.pallas_call(
        kernel,
        out_shape=(
            jax.ShapeDtypeStruct((rows_tok, width), BF),
            jax.ShapeDtypeStruct((rows_tok, width), BF),
            jax.ShapeDtypeStruct((2, rows_tok), F32),
            *(jax.ShapeDtypeStruct((1, *s), BF) for s in shapes),
        ),
        in_specs=[hbm] * 2 + [vmem] * 2 + [pl.BlockSpec(memory_space=pltpu.SMEM)] + [hbm] * 3,
        out_specs=tuple([vmem] * 6),
        scratch_shapes=[
            *([pltpu.VMEM((rows_tok, width), BF)] * 2),
            *(pltpu.VMEM((2 * nz, *s), BF) for s in shapes),
            pltpu.VMEM((ff, width), BF),
            *([block] * 4),
            pltpu.VMEM((slots, ff), BF),
            pltpu.VMEM((slots, 2 * ff), BF),
            *(pltpu.VMEM((2 * nz, *s), BF) for s in shapes),
            *(pltpu.VMEM((2, nz, *s), BF) for s in shapes),
            dma((2,)),
            dma((3,)),
            dma((3,)),
            dma((nz + 1, 3)),
            dma((3,)),
            dma((3,)),
            dma((2, nz, 3)),
            dma((3,)),
            dma((3,)),
            dma((NZL, 3)),
            dma,
            dma,
            dma,
            dma,
        ],
        compiler_params=pltpu.CompilerParams(
            collective_id=0, has_side_effects=True, vmem_limit_bytes=56 * 1024 * 1024
        ),
        cost_estimate=pl.CostEstimate(
            flops=flops, bytes_accessed=2 * 1024 * 1024, transcendentals=slots * ff
        ),
    )(
        tokens, cotangent, routing.T, gate_values.T, live_counts,
        gate_weights, up_weights, down_weights,
    )
    outs = pl.pallas_call(
        hand_over,
        out_shape=tuple(jax.ShapeDtypeStruct(o.shape, o.dtype) for o in outs),
        in_specs=[vmem] * len(outs),
        out_specs=tuple([vmem] * len(outs)),
    )(*outs)
    mixed, token_grad, gate_grad, grad_g, grad_u, grad_d = outs
    return mixed, token_grad, gate_grad.T, grad_g, grad_u, grad_d


def solution(mesh):
    return jax.shard_map(
        shards,
        mesh=mesh,
        in_specs=(
            P(("dp", "expert"), None),
            P(("dp", "expert"), None),
            P(("dp", "expert"), None),
            P(("dp", "expert"), None),
            P(("dp", "expert")),
            P("expert", "dp", None),
            P("expert", "dp", None),
            P("expert", "dp", None),
        ),
        out_specs=(
            P(("dp", "expert"), None),
            P(("dp", "expert"), None),
            P(("dp", "expert"), None),
            P("expert", "dp", None),
            P("expert", "dp", None),
            P("expert", "dp", None),
        ),
        check_vma=False,
    )
```
